32 devices in a mesh: stream: 8 (over y, x, core), shard: 4 (over z).
Axes of the slice: x: 2, y: 2, z: 4, core: 2. Of those that a mesh axis runs over, the one named last changes fastest.
Arguments:
- frames_in: bfloat16 [96, 4, 12, 5120], P('stream', None, None, 'shard'), may hold values from -6 to 6
- kept_state: float32 [96, 80, 64, 128], P('stream', 'shard'), may hold values from -6 to 6
- moved_to: int32 [96], P('stream'), may hold values from 0 to 95, as said below
- xz_weight: bfloat16 [5120, 2, 5120], P('stream', None, 'shard'), may hold values from -0.078125 to 0.078125
- side_weight: bfloat16 [5120, 336], P('stream'), may hold values from -0.01953125 to 0.01953125
- xz_mask: int32 [40, 2, 40], replicated, may hold values 0 or 1
- dt_bias: float32 [80], P('shard'), may hold values from -1 to 1
- decay_rate: float32 [80], P('shard'), may hold values from 0.00625 to 0.25
- skip_gain: float32 [80], P('shard'), may hold values from 0.5 to 1.5
- norm_gain: float32 [5120], P('shard'), may hold values from 0.1 to 1.9
- out_weight: bfloat16 [5120, 5120], P('stream', 'shard'), may hold values from -0.078125 to 0.078125
- out_mask: int32 [40, 40], replicated, may hold values 0 or 1
Outputs:
- mixed: bfloat16 [96, 4, 12, 5120], P('stream', None, None, 'shard')
- carry_state: float32 [96, 80, 64, 128], P('stream', 'shard')
The draws below stay inside these ranges and needn't reach their ends.
Inputs may be any that keep to these rules, and one draw needn't show every extreme that they name: `moved_to`: A permutation of the slots; the 12 old slots of index i of stream go, exactly 3 each, to the 4 indices i + 1, i + 2, i + 3 and i + 4 of stream (counted modulo 8).
All inputs are finite; a program needn't handle non-finite values.
Results may differ from the reference program's by a relative error of at most 0.025.
Values may be sent and summed in bfloat16 or wider, within the bound.
No kernel may reach another device: no remote copies, remote signals or barrier semaphores. Data moves between devices by JAX's collectives and lax.ppermute only.
A program may use at most 192 MiB of HBM per device.

```python
import math
import jax
import jax.numpy as jnp
from jax import lax

D = 5120
HEADS = 80
HEADDIM = 64
NSTATE = 128
NORM_GROUPS = 16
BLOCK = 128
FRAMES = 4
STREAM_DEV = 12
MOST = 3
PATCH = 12
DINNER = 5120
STREAMS = 96
N_SHARD = 4


def draw_moved_to(key, part):
    device_count = STREAMS // STREAM_DEV
    reach_count = STREAM_DEV // MOST
    first_key, second_key = jax.random.split(key)
    send_order = jax.vmap(lambda sub_key: jax.random.permutation(sub_key, STREAM_DEV))(jax.random.split(first_key, device_count))
    land_order = jax.vmap(lambda sub_key: jax.random.permutation(sub_key, STREAM_DEV))(jax.random.split(second_key, device_count))
    slot_ids = jnp.arange(STREAMS)
    source = slot_ids // STREAM_DEV
    within = slot_ids % STREAM_DEV
    rank_here = send_order[source, within]
    step_index = 1 + rank_here // MOST
    distance = jnp.where(step_index < reach_count, step_index, device_count // 2)
    target = (source + distance) % device_count
    landing_index = (step_index - 1) * MOST + rank_here % MOST
    new_within = land_order[target, landing_index]
    return (target * STREAM_DEV + new_within).astype(jnp.int32)


def place_ends(values, key, least, top_value):
    longest = values.shape.index(max(values.shape))
    spots = []
    for shift in (0, 1):
        where = [jax.random.randint(jax.random.fold_in(key, axis), (), 0, length) for axis, length in enumerate(values.shape)]
        where[longest] = (where[longest] + shift) % values.shape[longest]
        spots.append(tuple(where))
    return values.at[spots[0]].set(least).at[spots[1]].set(top_value)


def shard_levels(stream_key, dims, cuts, least, top_value):
    factor_of, own = 1.0, jax.random.fold_in(stream_key, 6)
    for position, shards_of in cuts:
        heights = jnp.exp(jax.random.uniform(jax.random.fold_in(own, position), (shards_of,), jnp.float32, least / len(cuts), top_value / len(cuts)))
        factor_of = factor_of * jnp.repeat(heights, dims[position] // shards_of).reshape([-1 if axis == position else 1 for axis in range(len(dims))])
    return factor_of


def centred(own_key, dims, deviation, most, shards=(), dtype=jnp.bfloat16):
    values = deviation * jax.random.normal(own_key, dims, jnp.float32)
    if shards:
        values = values * shard_levels(own_key, dims, shards, -0.22, 0.18)
    return jnp.clip(values, -most, most).astype(dtype)


def setup_inputs(seed: int = 0) -> dict:
    seeds = jax.random.split(jax.random.key(seed), 13)
    return {
        "frames_in": centred(seeds[0], (STREAMS, FRAMES, PATCH, D), 1.0, 6.0, ((0, 8), (3, 4))),
        "kept_state": centred(seeds[1], (STREAMS, HEADS, HEADDIM, NSTATE), 1.0, 6.0, ((0, 8), (1, 4)), jnp.float32),
        "moved_to": draw_moved_to(jax.random.fold_in(seeds[12], 71), 0),
        "xz_weight": centred(seeds[3], (D, 2, DINNER), D ** -0.5, 0.078125, ((0, 8), (2, 4))),
        "side_weight": centred(seeds[4], (D, 2 * NSTATE + HEADS), (D * NSTATE // 8) ** -0.5, 0.01953125, ((0, 8),)),
        "xz_mask": place_ends((jax.random.randint(seeds[5], (D // BLOCK, 2, DINNER // BLOCK), 0, 2) < 1).astype(jnp.int32), jax.random.fold_in(seeds[5], 1), 0, 1),
        "dt_bias": jnp.clip(jax.random.uniform(seeds[6], (HEADS,), jnp.float32, -1.0, 1.0) * shard_levels(seeds[6], (HEADS,), ((0, 4),), -0.4, 0.0), -1.0, 1.0),
        "decay_rate": jnp.clip(jnp.exp(math.log(0.25) - 3.6888794 * jax.random.uniform(seeds[7], (HEADS,), jnp.float32) ** shard_levels(seeds[7], (HEADS,), ((0, 4),), -0.2, 0.2)), 0.00625, 0.25),
        "skip_gain": jnp.clip(0.5 + 1.0 * jax.random.uniform(seeds[8], (HEADS,), jnp.float32) ** shard_levels(seeds[8], (HEADS,), ((0, 4),), -0.2, 0.2), 0.5, 1.5),
        "norm_gain": jnp.clip(1.0 + 0.18 * jax.random.normal(seeds[9], (DINNER,), jnp.float32), 0.1, 1.9),
        "out_weight": centred(seeds[10], (D, DINNER), DINNER ** -0.5, 0.078125, ((0, 8), (1, 4))),
        "out_mask": place_ends((jax.random.randint(seeds[11], (D // BLOCK, DINNER // BLOCK), 0, 2) < 1).astype(jnp.int32), jax.random.fold_in(seeds[11], 1), 0, 1),
    }


def frame_step(head_inputs, input_mix, output_mix, step_sizes, decay_rate, skip_gain, carry_state):
    highest = lax.Precision.HIGHEST
    length = head_inputs.shape[1]
    decays = -decay_rate * step_sizes
    cumulative = jnp.cumsum(decays, axis=1)
    causal = (jnp.arange(length)[:, None] >= jnp.arange(length)[None, :])[None, :, :, None]
    between = cumulative[:, :, None, :] - cumulative[:, None, :, :]
    weights = jnp.where(causal, jnp.exp(jnp.where(causal, between, 0.0)), 0.0)
    scores = jnp.einsum('sln,smn->slm', output_mix, input_mix, precision=highest)
    mixing = scores[:, :, :, None] * weights * step_sizes[:, None, :, :]
    inside = jnp.einsum('slmh,smhp->slhp', mixing, head_inputs, precision=highest)
    carried = jnp.exp(cumulative)[:, :, :, None] * jnp.einsum('sln,shpn->slhp', output_mix, carry_state, precision=highest)
    outputs = inside + carried + skip_gain[None, None, :, None] * head_inputs
    to_end = jnp.exp(cumulative[:, -1:, :] - cumulative) * step_sizes
    carry_state = jnp.exp(cumulative[:, -1, :])[:, :, None, None] * carry_state + jnp.einsum('slh,slhp,sln->shpn', to_end, head_inputs, input_mix, precision=highest)
    return (outputs, carry_state)

def reference(frames_in, kept_state, moved_to, xz_weight, side_weight, xz_mask, dt_bias, decay_rate, skip_gain, norm_gain, out_weight, out_mask):
    carry_state = jnp.zeros_like(kept_state).at[moved_to].set(kept_state)
    features = frames_in.reshape(-1, D)
    xz_full = jnp.repeat(jnp.repeat(xz_mask, BLOCK, axis=0), BLOCK, axis=2).astype(jnp.bfloat16)
    xz_total = jnp.dot(features, (xz_weight * xz_full).reshape(D, 2 * DINNER), preferred_element_type=jnp.float32)
    side_total = jnp.dot(features, side_weight, preferred_element_type=jnp.float32)
    head_inputs = xz_total[:, :DINNER].reshape(STREAMS, FRAMES, PATCH, HEADS, HEADDIM)
    gate_inputs = xz_total[:, DINNER:]
    input_mix = side_total[:, :NSTATE].reshape(STREAMS, FRAMES, PATCH, NSTATE)
    output_mix = side_total[:, NSTATE:2 * NSTATE].reshape(STREAMS, FRAMES, PATCH, NSTATE)
    step_sizes = jax.nn.softplus(side_total[:, 2 * NSTATE:] + dt_bias).reshape(STREAMS, FRAMES, PATCH, HEADS)
    results = []
    for frame_index in range(FRAMES):
        outputs, carry_state = frame_step(head_inputs[:, frame_index], input_mix[:, frame_index], output_mix[:, frame_index], step_sizes[:, frame_index], decay_rate, skip_gain, carry_state)
        results.append(outputs)
    row_count = features.shape[0]
    scanned = jnp.stack(results, axis=1).reshape(row_count, DINNER)
    gated = (scanned * jax.nn.silu(gate_inputs)).reshape(row_count, NORM_GROUPS, DINNER // NORM_GROUPS)
    mean_square = lax.optimization_barrier(jnp.mean(gated * gated, axis=2, keepdims=True))
    normed = ((gated * lax.rsqrt(mean_square + 1e-05)).reshape(row_count, DINNER) * norm_gain).astype(jnp.bfloat16)
    out_full = jnp.repeat(jnp.repeat(out_mask, BLOCK, axis=0), BLOCK, axis=1).astype(jnp.bfloat16)
    masked_out = out_weight * out_full
    group_width = DINNER // N_SHARD
    mixed = jnp.zeros((row_count, D), jnp.float32)
    for shard_index in range(N_SHARD):
        low = shard_index * group_width
        partial_term = jnp.dot(normed[:, low:low + group_width], masked_out[:, low:low + group_width].T, preferred_element_type=jnp.float32)
        rounded = lax.optimization_barrier(partial_term.astype(jnp.bfloat16))
        mixed = mixed + rounded.astype(jnp.float32)
    return (mixed.astype(jnp.bfloat16).reshape(STREAMS, FRAMES, PATCH, D), carry_state)
```

```python
import functools

import jax
import jax.numpy as jnp
from jax import lax
from jax.experimental import pallas as pl
from jax.experimental.pallas import tpu as pltpu
from jax.sharding import PartitionSpec as P

NSTATE = 128
NORM_GROUPS = 16
BLOCK = 128
FRAMES = 4
MOST = 3
DINNER = 5120


def frame_step(head_inputs, input_mix, output_mix, step_sizes, decay_rate, skip_gain, carry_state):
    highest = lax.Precision.HIGHEST
    length = head_inputs.shape[1]
    decays = -decay_rate * step_sizes
    cumulative = jnp.cumsum(decays, axis=1)
    causal = (jnp.arange(length)[:, None] >= jnp.arange(length)[None, :])[None, :, :, None]
    between = cumulative[:, :, None, :] - cumulative[:, None, :, :]
    weights = jnp.where(causal, jnp.exp(jnp.where(causal, between, 0.0)), 0.0)
    scores = jnp.einsum("sln,smn->slm", output_mix, input_mix, precision=highest)
    mixing = scores[:, :, :, None] * weights * step_sizes[:, None, :, :]
    inside = jnp.einsum("slmh,smhp->slhp", mixing, head_inputs, precision=highest)
    carried = jnp.exp(cumulative)[:, :, :, None] * jnp.einsum(
        "sln,shpn->slhp", output_mix, carry_state, precision=highest
    )
    outputs = inside + carried + skip_gain[None, None, :, None] * head_inputs
    to_end = jnp.exp(cumulative[:, -1:, :] - cumulative) * step_sizes
    carry_state = jnp.exp(cumulative[:, -1, :])[:, :, None, None] * carry_state + jnp.einsum(
        "slh,slhp,sln->shpn", to_end, head_inputs, input_mix, precision=highest
    )
    return (outputs, carry_state)


def column_table(column_ids, block_total):
    return (jnp.arange(block_total)[:, None] == (column_ids // BLOCK)[None, :]).astype(jnp.float32)


def row_table(panel_rows, block_rows):
    row_ids = jnp.arange(panel_rows)
    return ((row_ids // BLOCK)[:, None] == jnp.arange(block_rows)[None, :]).astype(jnp.float32)


def general(
    frames_in,
    kept_state,
    moved_to,
    xz_weight,
    side_weight,
    xz_mask,
    dt_bias,
    decay_rate,
    skip_gain,
    norm_gain,
    out_weight,
    out_mask,
):
    device_count = lax.axis_size("stream")
    shard_pos = lax.axis_index("shard")
    slots = kept_state.shape[0]
    target_dev = moved_to // slots
    target_slot = moved_to % slots
    slot_ids = jnp.arange(slots)
    same_dest = (target_dev[:, None] == target_dev[None, :]) & (
        slot_ids[:, None] > slot_ids[None, :]
    )
    ranking = jnp.sum(same_dest.astype(jnp.int32), axis=1)
    position = target_dev * MOST + ranking
    send_states = (
        jnp.zeros((device_count * MOST,) + kept_state.shape[1:], jnp.float32)
        .at[position]
        .set(kept_state)
    )
    send_slots = jnp.full((device_count * MOST,), -1, jnp.int32).at[position].set(target_slot)
    got_states, got_slots = (
        lax.all_to_all(
            send_states.astype(jnp.bfloat16), "stream", split_axis=0, concat_axis=0, tiled=True
        ).astype(send_states.dtype),
        lax.all_to_all(send_slots, "stream", split_axis=0, concat_axis=0, tiled=True),
    )
    landing = jnp.where(got_slots >= 0, got_slots, slots)
    carry_state = jnp.zeros_like(kept_state).at[landing].set(got_states, mode="drop")
    patch_len = frames_in.shape[2]
    local_rows = frames_in.reshape(-1, frames_in.shape[3])
    features = lax.all_gather(local_rows, "shard", axis=1, tiled=True)
    row_count = features.shape[0]
    width_local = xz_weight.shape[2]
    block_rows = xz_mask.shape[0]
    column_ids = shard_pos * width_local + jnp.arange(width_local)
    col_onehot = column_table(column_ids, xz_mask.shape[2])
    xz_keep = jnp.einsum("rgc,cl->rgl", xz_mask.astype(jnp.float32), col_onehot).reshape(
        block_rows, 2 * width_local
    )
    out_keep = jnp.dot(out_mask.astype(jnp.float32), col_onehot)
    panel = lax.all_gather(xz_weight, "stream", axis=0, tiled=True)
    panel_rows = panel.shape[0]
    keep_mask = jnp.dot(row_table(panel_rows, block_rows), xz_keep).astype(jnp.bfloat16)
    masked = panel.reshape(panel_rows, 2 * width_local) * keep_mask
    columns = features
    xz_total = jnp.dot(columns, masked, preferred_element_type=jnp.float32)
    columns = features
    side_total = jnp.dot(
        columns,
        lax.all_gather(side_weight, "stream", axis=0, tiled=True),
        preferred_element_type=jnp.float32,
    )
    head_count = dt_bias.shape[0]
    head_size = width_local // head_count
    head_inputs = xz_total[:, :width_local].reshape(slots, FRAMES, patch_len, head_count, head_size)
    gate_inputs = xz_total[:, width_local:]
    input_mix = side_total[:, :NSTATE].reshape(slots, FRAMES, patch_len, NSTATE)
    output_mix = side_total[:, NSTATE : 2 * NSTATE].reshape(slots, FRAMES, patch_len, NSTATE)
    step_raw = lax.dynamic_slice_in_dim(
        side_total, 2 * NSTATE + shard_pos * head_count, head_count, 1
    )
    step_sizes = jax.nn.softplus(step_raw + dt_bias).reshape(slots, FRAMES, patch_len, head_count)
    results = []
    for frame_index in range(FRAMES):
        outputs, carry_state = frame_step(
            head_inputs[:, frame_index],
            input_mix[:, frame_index],
            output_mix[:, frame_index],
            step_sizes[:, frame_index],
            decay_rate,
            skip_gain,
            carry_state,
        )
        results.append(outputs)
    scanned = jnp.stack(results, axis=1).reshape(row_count, width_local)
    gated = (scanned * jax.nn.silu(gate_inputs)).reshape(row_count, -1, DINNER // NORM_GROUPS)
    mean_square = jnp.mean(gated * gated, axis=2, keepdims=True)
    normed = (
        (gated * lax.rsqrt(mean_square + 1e-05)).reshape(row_count, width_local) * norm_gain
    ).astype(jnp.bfloat16)
    panel = lax.all_gather(out_weight, "stream", axis=0, tiled=True)
    panel_rows = panel.shape[0]
    keep_mask = jnp.dot(row_table(panel_rows, block_rows), out_keep).astype(jnp.bfloat16)
    partial_out = lax.dot_general(
        normed, panel * keep_mask, (((1,), (1,)), ((), ())), preferred_element_type=jnp.float32
    )
    mixed = lax.psum_scatter(
        partial_out.astype(jnp.bfloat16), "shard", scatter_dimension=1, tiled=True
    )
    return (mixed.reshape(slots, FRAMES, patch_len, -1), carry_state)


HEADDIM = 64
XZ_SHARE = 0.66
OUT_SHARE = 0.72
BF16 = jnp.bfloat16
F32 = jnp.float32
MIB = 1 << 20


def params(limit=48 * MIB):
    return pltpu.CompilerParams(vmem_limit_bytes=limit)


def cost(flops, nbytes):
    return pl.CostEstimate(flops=int(flops), bytes_accessed=int(nbytes), transcendentals=0)


def dot_f32(left, right):
    return jnp.dot(left, right, precision=lax.Precision.HIGHEST, preferred_element_type=F32)


def dot_nt(left, right):
    return lax.dot_general(left, right, (((1,), (1,)), ((), ())), preferred_element_type=F32)


def pack_kernel(half, block_rows, groups, columns, mask_columns, at_ref, mask_ref, x_ref, a_ref, b_ref):
    panel, shard = at_ref[0], at_ref[1]
    count = jnp.int32(0)
    for row in range(block_rows):
        for group in range(groups):
            for column in range(columns):
                place = ((panel * block_rows + row) * groups + group) * mask_columns + shard * columns + column
                keep = mask_ref[place] != 0
                low = (group * columns + column) * BLOCK
                rows = slice(row * BLOCK, (row + 1) * BLOCK)

                @pl.when(keep & (count < half))
                def _(count=count, low=low, rows=rows):
                    a_ref[count] = x_ref[rows, low : low + BLOCK]

                @pl.when(keep & (count >= half))
                def _(count=count, low=low, rows=rows):
                    b_ref[count - half] = x_ref[rows, low : low + BLOCK]

                count = count + keep.astype(jnp.int32)


def pack(at, mask, panel, groups, half):
    rows, width = panel.shape
    columns = width // groups // BLOCK
    mask_columns = mask.shape[-1]
    packed = jax.ShapeDtypeStruct((half, BLOCK, BLOCK), BF16)
    smem = pl.BlockSpec(memory_space=pltpu.SMEM)
    vmem = pl.BlockSpec(memory_space=pltpu.VMEM)
    return pl.pallas_call(
        functools.partial(pack_kernel, half, rows // BLOCK, groups, columns, mask_columns),
        out_shape=(packed, packed),
        in_specs=[smem, smem, vmem],
        out_specs=(vmem, vmem),
        compiler_params=params(),
        cost_estimate=cost(0, 2 * rows * width * 2),
    )(at, mask.reshape(-1), panel)


def spread_kernel(half, block_rows, groups, columns, mask_columns, at_ref, mask_ref, a_ref, b_ref, *rest):
    out_ref, count_ref = rest[-2:]
    row = pl.program_id(0)
    panel, shard = at_ref[0], at_ref[1]

    @pl.when(row == 0)
    def _():
        count_ref[0] = 0

    count = count_ref[0]
    for group in range(groups):
        for column in range(columns):
            place = ((panel * block_rows + row) * groups + group) * mask_columns + shard * columns + column
            keep = mask_ref[place] != 0
            low = (group * columns + column) * BLOCK

            @pl.when(keep & (count < half))
            def _(count=count, low=low):
                out_ref[0, :, low : low + BLOCK] = a_ref[count]

            @pl.when(keep & (count >= half))
            def _(count=count, low=low):
                out_ref[0, :, low : low + BLOCK] = b_ref[count - half]

            @pl.when(jnp.logical_not(keep))
            def _(low=low):
                out_ref[0, :, low : low + BLOCK] = jnp.zeros((BLOCK, BLOCK), BF16)

            count = count + keep.astype(jnp.int32)
    count_ref[0] = count


def spread(at, mask, a, b, groups, shape, before):
    _, rows, width = shape
    half = a.shape[0]
    columns = width // groups // BLOCK
    whole = pl.BlockSpec((half, BLOCK, BLOCK), lambda r, at, mask: (0, 0, 0))
    return pl.pallas_call(
        functools.partial(spread_kernel, half, rows // BLOCK, groups, columns, mask.shape[-1]),
        grid_spec=pltpu.PrefetchScalarGridSpec(
            num_scalar_prefetch=2,
            grid=(rows // BLOCK,),
            in_specs=[whole, whole] + ([] if before is None else [pl.BlockSpec(memory_space=pl.ANY)]),
            out_specs=pl.BlockSpec((1, BLOCK, width), lambda r, at, mask: (at[2], r, 0)),
            scratch_shapes=[pltpu.SMEM((1,), jnp.int32)],
        ),
        out_shape=jax.ShapeDtypeStruct(shape, BF16),
        input_output_aliases={} if before is None else {4: 0},
        compiler_params=params(),
        cost_estimate=cost(0, 3 * rows * width * 2),
    )(at, mask.reshape(-1), a, b, *(() if before is None else (before,)))


def product_kernel(count, *refs):
    base = refs[2 * count] if len(refs) > 2 * count + 1 else None
    total = jnp.zeros(refs[-1].shape, F32) if base is None else base[...]
    for step in range(count):
        total = total + jnp.dot(refs[step][...], refs[count + step][0], preferred_element_type=F32)
    refs[-1][...] = total


def product(features, dense, first, base, tile=256):
    count = len(features)
    rows, depth = features[0].shape
    width = dense.shape[2]
    out = pl.BlockSpec((rows, tile), lambda n: (0, n))
    return pl.pallas_call(
        functools.partial(product_kernel, count),
        grid=(width // tile,),
        in_specs=[pl.BlockSpec((rows, depth), lambda n: (0, 0))] * count
        + [pl.BlockSpec((1, depth, tile), lambda n, i=i: (first + i, 0, n)) for i in range(count)]
        + ([] if base is None else [out]),
        out_specs=out,
        out_shape=jax.ShapeDtypeStruct((rows, width), F32),
        input_output_aliases={} if base is None else {2 * count: 0},
        compiler_params=params(),
        cost_estimate=cost(2 * rows * depth * width * count, count * depth * width * 2 + 8 * rows * width),
    )(*features, *([dense] * count), *(() if base is None else (base,)))


def side_kernel(count, per, at_ref, side_ref, *refs):
    total = jnp.zeros(refs[-1].shape, F32)
    depth = side_ref.shape[2]
    for step in range(count):
        plane = lax.rem(at_ref[1] + (count - step), count)
        for part in range(per):
            total = total + dot_nt(refs[step][:, part * depth : (part + 1) * depth], side_ref[plane * per + part])
    refs[-1][...] = total


def side_product(at, side, features):
    count, (rows, width) = len(features), features[0].shape
    smem = pl.BlockSpec(memory_space=pltpu.SMEM)
    vmem = pl.BlockSpec(memory_space=pltpu.VMEM)
    columns = side.shape[1]
    return pl.pallas_call(
        functools.partial(side_kernel, count, side.shape[0] // count),
        in_specs=[smem, vmem] + [vmem] * count,
        out_specs=vmem,
        out_shape=jax.ShapeDtypeStruct((rows, columns), F32),
        compiler_params=params(),
        cost_estimate=cost(2 * rows * width * count * columns, count * width * (rows + columns) * 2),
    )(at, side, *features)


def pick_kernel(order_ref, x_ref, out_ref):
    out_ref[...] = x_ref[...].astype(out_ref.dtype)


def pick(order, states):
    count, block = order.shape[0], (1,) + states.shape[1:]
    return pl.pallas_call(
        pick_kernel,
        grid_spec=pltpu.PrefetchScalarGridSpec(
            num_scalar_prefetch=1,
            grid=(count,),
            in_specs=[pl.BlockSpec(block, lambda i, order: (order[i], 0, 0))],
            out_specs=pl.BlockSpec(block, lambda i, order: (i, 0, 0)),
        ),
        out_shape=jax.ShapeDtypeStruct((count,) + states.shape[1:], BF16),
        compiler_params=params(),
        cost_estimate=cost(0, count * states.shape[1] * states.shape[2] * 6),
    )(order, states)


def scan_kernel(heads, group_width, slots_ref, xz_ref, side_ref, state_ref, rows_ref, pick_ref, *rest):
    normed_ref, carry_ref = rest[-2:]
    length, width = normed_ref.shape
    head_inputs = xz_ref[:, :width]
    gate_inputs = xz_ref[:, width:]
    input_mix = side_ref[:, :NSTATE].astype(BF16)
    output_mix = side_ref[:, NSTATE : 2 * NSTATE].astype(BF16)
    bias, decay, skip, gain = (rows_ref[i : i + 1, :] for i in range(4))
    raw = dot_f32(side_ref[:, 2 * NSTATE :], pick_ref[...]) + bias
    steps = jnp.maximum(raw, 0.0) + jnp.log1p(jnp.exp(-jnp.abs(raw)))
    token = lax.broadcasted_iota(jnp.int32, (length, length), 0)
    earlier = lax.broadcasted_iota(jnp.int32, (length, length), 1)
    lower = (token >= earlier).astype(F32)
    cumulative = dot_f32(lower, -(steps * decay))
    lane = lax.broadcasted_iota(jnp.int32, (length, width), 1) & (HEADDIM - 1)
    line = lax.broadcasted_iota(jnp.int32, (length, width), 0)
    own = lane == line
    cum_row = jnp.sum(jnp.where(own, cumulative, 0.0), axis=0, keepdims=True)
    step_row = jnp.sum(jnp.where(own, steps, 0.0), axis=0, keepdims=True)
    last = cumulative[length - 1 : length, :]
    mixing = jnp.exp(jnp.where(lane <= line, cumulative - cum_row, -1e30)) * step_row
    half = lax.broadcasted_iota(jnp.int32, (length, 2 * HEADDIM), 1) < HEADDIM
    spare = jnp.zeros((HEADDIM - length, NSTATE), BF16)
    twice = jnp.concatenate([input_mix, spare, input_mix, spare], axis=0)
    scores = dot_nt(output_mix, twice)
    inputs16 = head_inputs.astype(BF16)
    inside = []
    for pair in range(heads // 2):
        low = pair * 2 * HEADDIM
        inputs = inputs16[:, low : low + 2 * HEADDIM]
        zero = jnp.zeros_like(inputs)
        pad = jnp.zeros((HEADDIM - length, 2 * HEADDIM), BF16)
        both = jnp.concatenate([jnp.where(half, inputs, zero), pad, jnp.where(half, zero, inputs), pad], axis=0)
        mix = (mixing[:, low : low + 2 * HEADDIM] * scores).astype(BF16)
        inside.append(jnp.dot(mix, both, preferred_element_type=F32))
    inside = jnp.concatenate(inside, axis=1)
    state = state_ref[0]
    carried = jnp.exp(cumulative) * dot_nt(output_mix, state)
    scanned = inside + carried + skip * head_inputs
    gated = scanned * (gate_inputs / (1.0 + jnp.exp(-gate_inputs)))
    channel = lax.broadcasted_iota(jnp.int32, (width, 128), 0)
    member = lax.broadcasted_iota(jnp.int32, (width, 128), 1) * group_width
    member = ((channel >= member) & (channel < member + group_width)).astype(BF16)
    squares = jnp.dot((gated * gated).astype(BF16), member, preferred_element_type=F32)
    scale = lax.rsqrt(squares * (1.0 / group_width) + 1e-05)
    position = lax.broadcasted_iota(jnp.int32, (length, width), 1)
    spread_scale = jnp.broadcast_to(scale[:, 0:1], (length, width))
    for group in range(1, width // group_width):
        spread_scale = jnp.where(position >= group * group_width, scale[:, group : group + 1], spread_scale)
    normed_ref[...] = (gated * spread_scale * gain).astype(BF16)
    to_end = (jnp.exp(last - cumulative) * steps * head_inputs).astype(BF16)
    added = lax.dot_general(to_end, input_mix, (((0,), (0,)), ((), ())), preferred_element_type=F32)
    head_rows = -(-heads // 8) * 8
    head_of = lax.broadcasted_iota(jnp.int32, (head_rows, width), 1)
    first = lax.broadcasted_iota(jnp.int32, (head_rows, width), 0) * HEADDIM
    whole = jnp.sum(jnp.where(head_of == first, last, 0.0), axis=1, keepdims=True)
    whole = jnp.broadcast_to(jnp.exp(whole), (head_rows, NSTATE))
    for head in range(heads):
        rows = slice(head * HEADDIM, (head + 1) * HEADDIM)
        carry_ref[0, rows, :] = state[rows].astype(F32) * whole[head : head + 1, :] + added[rows]


def scan(slots, xz, side, state, rows, picked, carry, total_slots, group_width):
    count, width, _ = state.shape
    length = xz.shape[0] // total_slots
    more = [] if carry is None else [pl.BlockSpec(memory_space=pl.ANY)]
    return pl.pallas_call(
        functools.partial(scan_kernel, width // HEADDIM, group_width),
        grid_spec=pltpu.PrefetchScalarGridSpec(
            num_scalar_prefetch=1,
            grid=(count,),
            in_specs=[
                pl.BlockSpec((length, 2 * width), lambda i, slots: (slots[i], 0)),
                pl.BlockSpec((length, side.shape[1]), lambda i, slots: (slots[i], 0)),
                pl.BlockSpec((1, width, NSTATE), lambda i, slots: (i, 0, 0)),
                pl.BlockSpec(rows.shape, lambda i, slots: (0, 0)),
                pl.BlockSpec(picked.shape, lambda i, slots: (0, 0)),
            ]
            + more,
            out_specs=(
                pl.BlockSpec((length, width), lambda i, slots: (i, 0)),
                pl.BlockSpec((1, width, NSTATE), lambda i, slots: (slots[i], 0, 0)),
            ),
        ),
        out_shape=(
            jax.ShapeDtypeStruct((count * length, width), BF16),
            jax.ShapeDtypeStruct((total_slots, width, NSTATE), F32),
        ),
        input_output_aliases={} if carry is None else {6: 1},
        compiler_params=params(),
        cost_estimate=cost(count * length * width * 1500, count * width * NSTATE * 6),
    )(slots, xz, side, state, rows, picked, *(() if carry is None else (carry,)))


def add_kernel(at_ref, normed_ref, out_ref, *rest):
    total = dot_nt(normed_ref[...], out_ref[0])
    if len(rest) > 1:
        total = total + rest[0][...].astype(F32)
    rest[-1][...] = total.astype(BF16)


def add_term(at, normed, dense, dest, shards, got):
    rows, depth = normed.shape
    width = dense.shape[1]
    whole = pl.BlockSpec((rows, width), lambda i, at: (0, 0))
    return pl.pallas_call(
        add_kernel,
        grid_spec=pltpu.PrefetchScalarGridSpec(
            num_scalar_prefetch=1,
            grid=(1,),
            in_specs=[
                pl.BlockSpec((rows, depth), lambda i, at: (0, 0)),
                pl.BlockSpec((1, width, depth), lambda i, at: (lax.rem(at[1] + (shards - dest), shards), 0, 0)),
            ]
            + ([] if got is None else [whole]),
            out_specs=whole,
        ),
        out_shape=jax.ShapeDtypeStruct((rows, width), BF16),
        compiler_params=params(),
        cost_estimate=cost(2 * rows * depth * width, width * depth * 2),
    )(at, normed, dense, *(() if got is None else (got,)))


def place_kernel(frames, at_ref, slots_ref, normed_ref, dense_ref, got_ref, *rest):
    out_ref = rest[-1]
    total = (dot_nt(normed_ref[...], dense_ref[0]) + got_ref[...].astype(F32)).astype(BF16).astype(F32)
    patch = total.shape[0] // frames
    for frame in range(frames):
        out_ref[0, frame] = total[frame * patch : (frame + 1) * patch].astype(BF16)


def place_term(at, slots, normed, dense, got, total_slots, before):
    rows, depth = normed.shape
    count = slots.shape[0]
    length = rows // count
    width = dense.shape[1]
    patch = length // FRAMES
    return pl.pallas_call(
        functools.partial(place_kernel, FRAMES),
        grid_spec=pltpu.PrefetchScalarGridSpec(
            num_scalar_prefetch=2,
            grid=(count,),
            in_specs=[
                pl.BlockSpec((length, depth), lambda i, at, slots: (i, 0)),
                pl.BlockSpec((1, width, depth), lambda i, at, slots: (at[1], 0, 0)),
                pl.BlockSpec((length, width), lambda i, at, slots: (i, 0)),
            ]
            + ([] if before is None else [pl.BlockSpec(memory_space=pl.ANY)]),
            out_specs=pl.BlockSpec((1, FRAMES, patch, width), lambda i, at, slots: (slots[i], 0, 0, 0)),
        ),
        out_shape=jax.ShapeDtypeStruct((total_slots, FRAMES, patch, width), BF16),
        input_output_aliases={} if before is None else {5: 0},
        compiler_params=params(),
        cost_estimate=cost(2 * rows * depth * width, width * depth * 2),
    )(at, slots, normed, dense, got, *(() if before is None else (before,)))


def swap(value, bit, size):
    return lax.ppermute(value, "stream", [(i, i ^ bit) for i in range(size)])


def cube(halves, size):
    a, b = halves
    got_a, got_b = {0: a}, {0: b}
    got_a[2], got_a[4] = swap(a, 2, size), swap(a, 4, size)
    got_b[2], got_b[4] = swap(b, 2, size), swap(b, 4, size)
    got_a[6] = swap(got_a[4], 2, size)
    got_b[6] = swap(got_b[2], 4, size)
    for bits in (0, 2, 4, 6):
        got_a[bits | 1] = swap(got_a[bits], 1, size)
        got_b[bits | 1] = swap(got_b[bits], 1, size)
    return got_a, got_b


def after(values, earlier):
    return lax.optimization_barrier((values, earlier))[0]


def sparse(
    xz_room,
    out_room,
    frames_in,
    kept_state,
    moved_to,
    xz_weight,
    side_weight,
    xz_mask,
    dt_bias,
    decay_rate,
    skip_gain,
    norm_gain,
    out_weight,
    out_mask,
):
    streams, shards = lax.axis_size("stream"), lax.axis_size("shard")
    me, shard = lax.axis_index("stream"), lax.axis_index("shard")
    at = jnp.stack([me, shard, jnp.zeros_like(me)]).astype(jnp.int32)
    slots, heads = kept_state.shape[:2]
    width = heads * HEADDIM
    ring = [(i, (i + 1) % shards) for i in range(shards)]

    features = [frames_in.reshape(-1, frames_in.shape[3])]
    for _ in range(shards - 1):
        features.append(lax.ppermute(features[-1], "shard", ring))

    xz_panel = xz_weight.reshape(xz_weight.shape[0], -1)
    xz_halves = pack(at, xz_mask, xz_panel, 2, xz_room // 2)
    out_halves = pack(at, out_mask, out_weight, 1, out_room // 2)
    xz_a, xz_b = cube(xz_halves, streams)
    side = lax.all_gather(side_weight.T, "stream", axis=0)

    steps = (1, 2, 3, streams // 2)
    distance = (moved_to // slots - me) % streams
    match = distance[None, :] == jnp.array(steps)[:, None]
    rank = jnp.cumsum(match.astype(jnp.int32), axis=1) - 1
    chosen = match[:, None, :] & (rank[:, None, :] == jnp.arange(MOST)[None, :, None])
    order = jnp.sum(jnp.where(chosen, jnp.arange(slots), 0), axis=2, dtype=jnp.int32)
    landing = jnp.sum(jnp.where(chosen, moved_to % slots, 0), axis=2, dtype=jnp.int32)
    flat_state = kept_state.reshape(slots, width, NSTATE)
    sends = [pick(order[k], flat_state) for k in range(len(steps))]
    sends = after(sends, (xz_a[6], xz_b[6]))
    got_states, got_slots = [], []
    for k, step in enumerate(steps):
        pairs = [(i, (i + step) % streams) for i in range(streams)]
        got_states.append(lax.ppermute(sends[k], "stream", pairs))
        got_slots.append(lax.ppermute(landing[k], "stream", pairs))
    out_halves = after(out_halves, (xz_a[6], xz_b[6]))
    out_a, out_b = cube(out_halves, streams)

    per = streams // shards
    dense = None
    for bits in range(streams):
        panel = me ^ bits
        where = (shard - panel // per) % shards * per + panel % per
        spot = jnp.stack([panel, shard, where]).astype(jnp.int32)
        dense = spread(spot, xz_mask, xz_a[bits], xz_b[bits], 2, (streams, *xz_panel.shape), dense)
    dense = dense.reshape(shards, -1, xz_panel.shape[1])
    out_dense = None
    for bits in range(streams):
        spot = jnp.stack([me ^ bits, shard, me ^ bits]).astype(jnp.int32)
        out_dense = spread(spot, out_mask, out_a[bits], out_b[bits], 1, (streams, *out_weight.shape), out_dense)
    out_dense = out_dense.reshape(shards, -1, width)

    xz = product(features[:-1], dense, 0, None)
    xz = product(features[-1:], dense, shards - 1, xz)
    side_total = side_product(at, side, features)
    head_of = jnp.arange(width) // HEADDIM
    picked = (shard * heads + head_of[None, :] == jnp.arange(heads * shards)[:, None]).astype(F32)
    per_head = [jnp.repeat(v, HEADDIM) for v in (dt_bias, decay_rate, skip_gain)]
    rows = jnp.stack(per_head + [norm_gain] + [jnp.zeros_like(norm_gain)] * 4)

    carry, mixed = None, None
    normed = []
    for k in range(len(steps)):
        done, carry = scan(
            got_slots[k], xz, side_total, got_states[k], rows, picked, carry, slots, DINNER // NORM_GROUPS
        )
        normed.append(done)
    for k in range(len(steps)):
        moving = None
        for hop in range(1, shards):
            moving = lax.ppermute(add_term(at, normed[k], out_dense, hop, shards, moving), "shard", ring)
        mixed = place_term(at, got_slots[k], normed[k], out_dense, moving, slots, mixed)
    return mixed, carry.reshape(kept_state.shape)


def fullest(mask, panels, shards):
    rows = mask.reshape(panels, -1, mask.shape[-1])
    cells = rows.reshape(panels, rows.shape[1], shards, -1)
    return jnp.max(jnp.sum(cells, axis=(1, 3)))


def on_device(streams, shards, *args):
    xz_weight, out_weight, kept_state = args[3], args[10], args[1]
    rows, width = out_weight.shape
    regular = (
        streams == 8
        and streams % shards == 0
        and rows % BLOCK == 0
        and width % BLOCK == 0
        and width % (DINNER // NORM_GROUPS) == 0
        and kept_state.shape[1] % 2 == 0
    )
    if not regular:
        return general(*args)
    blocks = (rows // BLOCK) * (width // BLOCK)
    xz_room = int(2 * blocks * XZ_SHARE) // 2 * 2
    out_room = int(blocks * OUT_SHARE) // 2 * 2
    fits = (fullest(args[5], streams, shards) <= xz_room) & (fullest(args[11], streams, shards) <= out_room)
    return lax.cond(
        fits,
        functools.partial(sparse, xz_room, out_room),
        functools.partial(sparse, 2 * blocks, blocks),
        *args,
    )


def solution(mesh):
    placed = (
        P("stream", None, None, "shard"),
        P("stream", "shard", None, None),
        P("stream"),
        P("stream", None, "shard"),
        P("stream", None),
        P(),
        P("shard"),
        P("shard"),
        P("shard"),
        P("shard"),
        P("stream", "shard"),
        P(),
    )
    return jax.shard_map(
        functools.partial(on_device, mesh.shape["stream"], mesh.shape["shard"]),
        mesh=mesh,
        in_specs=placed,
        out_specs=(P("stream", None, None, "shard"), P("stream", "shard", None, None)),
        check_vma=False,
    )
```

```python
import functools

import jax
import jax.numpy as jnp
from jax import lax
from jax.experimental import pallas as pl
from jax.experimental.pallas import tpu as pltpu
from jax.sharding import PartitionSpec as P

NSTATE = 128
NORM_GROUPS = 16
BLOCK = 128
FRAMES = 4
MOST = 3
DINNER = 5120


def frame_step(head_inputs, input_mix, output_mix, step_sizes, decay_rate, skip_gain, carry_state):
    highest = lax.Precision.HIGHEST
    length = head_inputs.shape[1]
    decays = -decay_rate * step_sizes
    cumulative = jnp.cumsum(decays, axis=1)
    causal = (jnp.arange(length)[:, None] >= jnp.arange(length)[None, :])[None, :, :, None]
    between = cumulative[:, :, None, :] - cumulative[:, None, :, :]
    weights = jnp.where(causal, jnp.exp(jnp.where(causal, between, 0.0)), 0.0)
    scores = jnp.einsum("sln,smn->slm", output_mix, input_mix, precision=highest)
    mixing = scores[:, :, :, None] * weights * step_sizes[:, None, :, :]
    inside = jnp.einsum("slmh,smhp->slhp", mixing, head_inputs, precision=highest)
    carried = jnp.exp(cumulative)[:, :, :, None] * jnp.einsum(
        "sln,shpn->slhp", output_mix, carry_state, precision=highest
    )
    outputs = inside + carried + skip_gain[None, None, :, None] * head_inputs
    to_end = jnp.exp(cumulative[:, -1:, :] - cumulative) * step_sizes
    carry_state = jnp.exp(cumulative[:, -1, :])[:, :, None, None] * carry_state + jnp.einsum(
        "slh,slhp,sln->shpn", to_end, head_inputs, input_mix, precision=highest
    )
    return (outputs, carry_state)


def column_table(column_ids, block_total):
    return (jnp.arange(block_total)[:, None] == (column_ids // BLOCK)[None, :]).astype(jnp.float32)


def row_table(panel_rows, block_rows):
    row_ids = jnp.arange(panel_rows)
    return ((row_ids // BLOCK)[:, None] == jnp.arange(block_rows)[None, :]).astype(jnp.float32)


def general(
    frames_in,
    kept_state,
    moved_to,
    xz_weight,
    side_weight,
    xz_mask,
    dt_bias,
    decay_rate,
    skip_gain,
    norm_gain,
    out_weight,
    out_mask,
):
    device_count = lax.axis_size("stream")
    shard_pos = lax.axis_index("shard")
    slots = kept_state.shape[0]
    target_dev = moved_to // slots
    target_slot = moved_to % slots
    slot_ids = jnp.arange(slots)
    same_dest = (target_dev[:, None] == target_dev[None, :]) & (
        slot_ids[:, None] > slot_ids[None, :]
    )
    ranking = jnp.sum(same_dest.astype(jnp.int32), axis=1)
    position = target_dev * MOST + ranking
    send_states = (
        jnp.zeros((device_count * MOST,) + kept_state.shape[1:], jnp.float32)
        .at[position]
        .set(kept_state)
    )
    send_slots = jnp.full((device_count * MOST,), -1, jnp.int32).at[position].set(target_slot)
    got_states, got_slots = (
        lax.all_to_all(
            send_states.astype(jnp.bfloat16), "stream", split_axis=0, concat_axis=0, tiled=True
        ).astype(send_states.dtype),
        lax.all_to_all(send_slots, "stream", split_axis=0, concat_axis=0, tiled=True),
    )
    landing = jnp.where(got_slots >= 0, got_slots, slots)
    carry_state = jnp.zeros_like(kept_state).at[landing].set(got_states, mode="drop")
    patch_len = frames_in.shape[2]
    local_rows = frames_in.reshape(-1, frames_in.shape[3])
    features = lax.all_gather(local_rows, "shard", axis=1, tiled=True)
    row_count = features.shape[0]
    width_local = xz_weight.shape[2]
    block_rows = xz_mask.shape[0]
    column_ids = shard_pos * width_local + jnp.arange(width_local)
    col_onehot = column_table(column_ids, xz_mask.shape[2])
    xz_keep = jnp.einsum("rgc,cl->rgl", xz_mask.astype(jnp.float32), col_onehot).reshape(
        block_rows, 2 * width_local
    )
    out_keep = jnp.dot(out_mask.astype(jnp.float32), col_onehot)
    panel = lax.all_gather(xz_weight, "stream", axis=0, tiled=True)
    panel_rows = panel.shape[0]
    keep_mask = jnp.dot(row_table(panel_rows, block_rows), xz_keep).astype(jnp.bfloat16)
    masked = panel.reshape(panel_rows, 2 * width_local) * keep_mask
    columns = features
    xz_total = jnp.dot(columns, masked, preferred_element_type=jnp.float32)
    columns = features
    side_total = jnp.dot(
        columns,
        lax.all_gather(side_weight, "stream", axis=0, tiled=True),
        preferred_element_type=jnp.float32,
    )
    head_count = dt_bias.shape[0]
    head_size = width_local // head_count
    head_inputs = xz_total[:, :width_local].reshape(slots, FRAMES, patch_len, head_count, head_size)
    gate_inputs = xz_total[:, width_local:]
    input_mix = side_total[:, :NSTATE].reshape(slots, FRAMES, patch_len, NSTATE)
    output_mix = side_total[:, NSTATE : 2 * NSTATE].reshape(slots, FRAMES, patch_len, NSTATE)
    step_raw = lax.dynamic_slice_in_dim(
        side_total, 2 * NSTATE + shard_pos * head_count, head_count, 1
    )
    step_sizes = jax.nn.softplus(step_raw + dt_bias).reshape(slots, FRAMES, patch_len, head_count)
    results = []
    for frame_index in range(FRAMES):
        outputs, carry_state = frame_step(
            head_inputs[:, frame_index],
            input_mix[:, frame_index],
            output_mix[:, frame_index],
            step_sizes[:, frame_index],
            decay_rate,
            skip_gain,
            carry_state,
        )
        results.append(outputs)
    scanned = jnp.stack(results, axis=1).reshape(row_count, width_local)
    gated = (scanned * jax.nn.silu(gate_inputs)).reshape(row_count, -1, DINNER // NORM_GROUPS)
    mean_square = jnp.mean(gated * gated, axis=2, keepdims=True)
    normed = (
        (gated * lax.rsqrt(mean_square + 1e-05)).reshape(row_count, width_local) * norm_gain
    ).astype(jnp.bfloat16)
    panel = lax.all_gather(out_weight, "stream", axis=0, tiled=True)
    panel_rows = panel.shape[0]
    keep_mask = jnp.dot(row_table(panel_rows, block_rows), out_keep).astype(jnp.bfloat16)
    partial_out = lax.dot_general(
        normed, panel * keep_mask, (((1,), (1,)), ((), ())), preferred_element_type=jnp.float32
    )
    mixed = lax.psum_scatter(
        partial_out.astype(jnp.bfloat16), "shard", scatter_dimension=1, tiled=True
    )
    return (mixed.reshape(slots, FRAMES, patch_len, -1), carry_state)


HEADDIM = 64
XZ_SHARE = 0.66
OUT_SHARE = 0.72
BF16 = jnp.bfloat16
F32 = jnp.float32
MIB = 1 << 20


def params(limit=48 * MIB):
    return pltpu.CompilerParams(vmem_limit_bytes=limit)


def cost():
    return pl.CostEstimate(flops=1, bytes_accessed=1, transcendentals=0)


def dot_nt(left, right):
    return lax.dot_general(left, right, (((1,), (1,)), ((), ())), preferred_element_type=F32)


def pack_kernel(block_rows, groups, columns, mask_columns, low_count, room, always, turn, at_ref, mask_ref, x_ref, *rest):
    out_ref = rest[-1]
    panel, shard = at_ref[0], at_ref[1]
    base = 0
    if low_count == 0:
        base = 1 + block_rows * always
        out_ref[0] = jnp.zeros((BLOCK, BLOCK), BF16)
        for row in range(block_rows):
            for column in range(always):
                block = rest[0][column * BLOCK : (column + 1) * BLOCK, row * BLOCK : (row + 1) * BLOCK].T
                short = BLOCK - block.shape[1]
                if short:
                    block = jnp.concatenate([block, jnp.zeros((BLOCK, short), BF16)], axis=1)
                out_ref[1 + row * always + column] = block
    count = jnp.int32(-low_count)
    for row in range(block_rows):
        for group in range(groups):
            for column in range(columns):
                place = ((panel * block_rows + row) * groups + group) * mask_columns + shard * columns + column
                keep = mask_ref[place] != 0
                low = (group * columns + column) * BLOCK

                @pl.when(keep & (count >= 0) & (count < room))
                def _(count=count, low=low, row=row):
                    block = x_ref[row * BLOCK : (row + 1) * BLOCK, low : low + BLOCK]
                    out_ref[base + count] = block.T if turn else block

                count = count + keep.astype(jnp.int32)


def pack(at, mask, panel, groups, low_count, room, turn, beside=None):
    rows, width = panel.shape
    columns = width // groups // BLOCK
    always = 0 if beside is None else -(-beside.shape[0] // BLOCK)
    smem = pl.BlockSpec(memory_space=pltpu.SMEM)
    vmem = pl.BlockSpec(memory_space=pltpu.VMEM)
    extra = () if beside is None else (beside,)
    size = room if low_count else 1 + rows // BLOCK * always + room
    return pl.pallas_call(
        functools.partial(
            pack_kernel, rows // BLOCK, groups, columns, mask.shape[-1], low_count, room, always, turn
        ),
        out_shape=jax.ShapeDtypeStruct((size, BLOCK, BLOCK), BF16),
        in_specs=[smem, smem, vmem] + [vmem] * len(extra),
        out_specs=vmem,
        compiler_params=params(),
        cost_estimate=cost(),
    )(at, mask.reshape(-1), panel, *extra)


def unwritten(shape):
    return pl.pallas_call(
        lambda out_ref: None,
        out_shape=jax.ShapeDtypeStruct(shape, BF16),
        out_specs=pl.BlockSpec(memory_space=pl.ANY),
        cost_estimate=cost(),
    )()


def slot_table(mask, panels, shard, shards, always):
    rows = mask.shape[0] // panels
    mine = lax.dynamic_slice_in_dim(mask, shard * (mask.shape[-1] // shards), mask.shape[-1] // shards, mask.ndim - 1)
    kept = mine.reshape(panels, -1)
    size = kept.shape[1]
    before = (jnp.arange(size)[:, None] < jnp.arange(size)[None, :]).astype(F32)
    rank = jnp.dot(kept.astype(F32), before).astype(jnp.int32)
    table = jnp.where(kept != 0, rank + 1 + rows * always, 0).reshape(panels, rows, -1)
    fixed = 1 + jnp.arange(rows)[:, None] * always + jnp.arange(always)[None, :]
    fixed = jnp.broadcast_to(fixed[None], (panels, rows, always)).astype(jnp.int32)
    return jnp.concatenate([table, fixed], axis=2).reshape(-1)


def panel_copies(parts, over, panel, held, sems):
    copies, low = [], 0
    for i, part in enumerate(parts):
        copies.append(pltpu.make_async_copy(part, held.at[pl.ds(low, part.shape[0])], sems.at[i]))
        low += part.shape[0]
    return copies, pltpu.make_async_copy(over.at[panel], held.at[pl.ds(low, over.shape[1])], sems.at[2])


def project_kernel(counts, block_rows, blocks, tiles, at_ref, table_ref, x_ref, over_ref, *refs):
    out_ref, held, x_held, *dense, total, sems, x_sems, out_sems = refs[len(refs) - 9 :]
    parts, low = [], 0
    for count in counts:
        parts.append(refs[low : low + count])
        low += count
    me, extra = at_ref[0], at_ref[2] != 0
    depth = block_rows * BLOCK
    pairs = len(counts) // 2

    def fetch(pair):
        slot, plain, more = pair % 2, [], []
        for side in range(2):
            panel = me ^ (2 * pair + side)
            copies, over = panel_copies(
                parts[2 * pair + side], over_ref, panel, held.at[slot, side], sems.at[slot, side]
            )
            columns = pl.ds(pl.multiple_of(panel * depth, BLOCK), depth)
            copies.append(
                pltpu.make_async_copy(
                    x_ref.at[:, columns], x_held.at[slot, :, pl.ds(side * depth, depth)], x_sems.at[slot, side]
                )
            )
            plain += copies
            more.append(over)
        return plain, more

    def start(pair):
        plain, more = fetch(pair)
        for copy in plain:
            copy.start()

        @pl.when(extra)
        def _():
            for copy in more:
                copy.start()

    def wait(pair):
        plain, more = fetch(pair)
        for copy in plain:
            copy.wait()

        @pl.when(extra)
        def _():
            for copy in more:
                copy.wait()

    def out_copy(n):
        first, size = tiles[n]
        columns = pl.ds(first * BLOCK, size * BLOCK)
        return pltpu.make_async_copy(total.at[:, columns], out_ref.at[:, columns], out_sems.at[n])

    def fill(pair, n):
        first, size = tiles[n]
        for side in range(2):
            panel = me ^ (2 * pair + side)
            for row in range(block_rows):
                line = (panel * block_rows + row) * blocks + first
                high = (side * block_rows + row) * BLOCK
                for column in range(size):
                    dense[n % 2][high : high + BLOCK, column * BLOCK : (column + 1) * BLOCK] = held[
                        pair % 2, side, table_ref[line + column]
                    ]

    def multiply(pair, n):
        first, size = tiles[n]
        columns = slice(first * BLOCK, (first + size) * BLOCK)
        term = jnp.dot(x_held[pair % 2], dense[n % 2][:, : size * BLOCK], preferred_element_type=F32)
        total[:, columns] = term + jnp.where(pair > 0, total[:, columns], 0.0)

    start(0)

    @pl.loop(0, pairs)
    def _(pair):
        for i in range(pairs):

            @pl.when(pair == i)
            def _(i=i):
                wait(i)
                if i + 1 < pairs:
                    start(i + 1)

        fill(pair, 0)
        for n in range(len(tiles)):
            if n + 1 < len(tiles):
                fill(pair, n + 1)
            multiply(pair, n)

            @pl.when(pair == pairs - 1)
            def _(n=n):
                out_copy(n).start()

    for n in range(len(tiles)):
        out_copy(n).wait()


def project(at, table, features, panels, over, block_rows, wide=4):
    rows = features.shape[0]
    count = len(panels)
    blocks = table.shape[0] // (count * block_rows)
    size = sum(part.shape[0] for part in panels[0]) + over.shape[1]
    flat = [part for bits in range(count) for part in panels[bits]]
    smem = pl.BlockSpec(memory_space=pltpu.SMEM)
    anywhere = pl.BlockSpec(memory_space=pl.ANY)
    depth = 2 * block_rows * BLOCK
    tiles = [(first, min(wide, blocks - first)) for first in range(0, blocks, wide)]
    return pl.pallas_call(
        functools.partial(project_kernel, [len(panels[b]) for b in range(count)], block_rows, blocks, tiles),
        out_shape=jax.ShapeDtypeStruct((rows, blocks * BLOCK), F32),
        in_specs=[smem, smem] + [anywhere] * (2 + len(flat)),
        out_specs=anywhere,
        scratch_shapes=[
            pltpu.VMEM((2, 2, size, BLOCK, BLOCK), BF16),
            pltpu.VMEM((2, rows, depth), BF16),
            pltpu.VMEM((depth, wide * BLOCK), BF16),
            pltpu.VMEM((depth, wide * BLOCK), BF16),
            pltpu.VMEM((rows, blocks * BLOCK), F32),
            pltpu.SemaphoreType.DMA((2, 2, 3)),
            pltpu.SemaphoreType.DMA((2, 2)),
            pltpu.SemaphoreType.DMA((len(tiles),)),
        ],
        compiler_params=params(56 * MIB),
        cost_estimate=cost(),
    )(at, table, features, over, *flat)


def expand_kernel(counts, first_pair, block_rows, blocks, at_ref, table_ref, over_ref, *refs):
    out_ref, held, sems = refs[len(refs) - 3 :]
    me, extra = at_ref[0], at_ref[2] != 0
    pairs = len(counts) // 2
    step = pl.program_id(0)

    def copies(pair):
        low = sum(counts[: 2 * pair])
        plain, more = [], []
        for side in range(2):
            parts = refs[low : low + counts[2 * pair + side]]
            low += counts[2 * pair + side]
            panel = me ^ (2 * (first_pair + pair) + side)
            some, over = panel_copies(parts, over_ref, panel, held.at[pair, side], sems.at[pair, side])
            plain += some
            more.append(over)
        return plain, more

    @pl.when(step == 0)
    def _():
        for pair in range(pairs):
            plain, more = copies(pair)
            for copy in plain:
                copy.start()

            @pl.when(extra)
            def _(more=more):
                for copy in more:
                    copy.start()

    for pair in range(pairs):

        @pl.when(step == pair)
        def _(pair=pair):
            plain, more = copies(pair)
            for copy in plain:
                copy.wait()

            @pl.when(extra)
            def _():
                for copy in more:
                    copy.wait()

    for side in range(2):
        panel = me ^ (2 * (first_pair + step) + side)
        place = (panel % 2) * (block_rows * BLOCK)
        for row in range(block_rows):
            columns = pl.ds(pl.multiple_of(place + row * BLOCK, BLOCK), BLOCK)
            line = (panel * block_rows + row) * blocks
            for column in range(blocks):
                out_ref[0, column * BLOCK : (column + 1) * BLOCK, columns] = held[step, side, table_ref[line + column]]


def expand(at, table, panels, over, first_pair, pairs, block_rows, before):
    count = over.shape[0]
    total_pairs = count // 2
    blocks = table.shape[0] // (count * block_rows)
    chosen = [panels[2 * first_pair + i] for i in range(2 * pairs)]
    flat = [part for parts in chosen for part in parts]
    size = sum(part.shape[0] for part in chosen[0]) + over.shape[1]
    anywhere = pl.BlockSpec(memory_space=pl.ANY)
    shape = (total_pairs, blocks * BLOCK, 2 * block_rows * BLOCK)
    more = [] if before is None else [before]
    return pl.pallas_call(
        functools.partial(expand_kernel, [len(parts) for parts in chosen], first_pair, block_rows, blocks),
        grid_spec=pltpu.PrefetchScalarGridSpec(
            num_scalar_prefetch=2,
            grid=(pairs,),
            in_specs=[anywhere] * (1 + len(flat) + len(more)),
            out_specs=pl.BlockSpec((1, *shape[1:]), lambda i, at, table: ((at[0] // 2) ^ (first_pair + i), 0, 0)),
            scratch_shapes=[
                pltpu.VMEM((pairs, 2, size, BLOCK, BLOCK), BF16),
                pltpu.SemaphoreType.DMA((pairs, 2, 3)),
            ],
        ),
        out_shape=jax.ShapeDtypeStruct(shape, BF16),
        input_output_aliases={3 + len(flat): 0} if more else {},
        compiler_params=params(),
        cost_estimate=cost(),
    )(at, table, over, *flat, *more)


def pick_kernel(order_ref, x_ref, out_ref):
    out_ref[...] = x_ref[...].astype(out_ref.dtype)


def pick(order, states):
    count, block = order.shape[0], (1,) + states.shape[1:]
    return pl.pallas_call(
        pick_kernel,
        grid_spec=pltpu.PrefetchScalarGridSpec(
            num_scalar_prefetch=1,
            grid=(count,),
            in_specs=[pl.BlockSpec(block, lambda i, order: (order[i], 0, 0))],
            out_specs=pl.BlockSpec(block, lambda i, order: (i, 0, 0)),
        ),
        out_shape=jax.ShapeDtypeStruct((count,) + states.shape[1:], BF16),
        compiler_params=params(),
        cost_estimate=cost(),
    )(order, states)


def split(values):
    high = values.astype(BF16)
    left = values - high.astype(F32)
    middle = left.astype(BF16)
    return high, middle, (left - middle.astype(F32)).astype(BF16)


def scan_kernel(heads, group_width, slots_ref, total_ref, state_ref, rows_ref, heads_ref, pick_ref, *rest):
    normed_ref, carry_ref = rest[-2:]
    length, width = normed_ref.shape
    head_inputs = total_ref[:, :width]
    gate_inputs = total_ref[:, width : 2 * width]
    side = 2 * width
    input_mix = total_ref[:, side : side + NSTATE].astype(BF16)
    output_mix = total_ref[:, side + NSTATE : side + 2 * NSTATE].astype(BF16)
    bias, decay = heads_ref[0:1, :], heads_ref[1:2, :]
    skip, gain = rows_ref[0:1, :], rows_ref[1:2, :]
    raw = total_ref[:, side + 2 * NSTATE : side + 2 * NSTATE + heads_ref.shape[1]] + bias
    steps = jnp.maximum(raw, 0.0) + jnp.log1p(jnp.exp(-jnp.abs(raw)))
    patch = length // FRAMES

    def token(shape, axis, size):
        row = lax.broadcasted_iota(jnp.int32, shape, axis) & (size - 1)
        return (row & (FRAMES - 1)) * patch + row // FRAMES

    square = (length, length)
    lower = (token(square, 0, 64) >= token(square, 1, 64)).astype(BF16)
    cumulative = sum(jnp.dot(lower, part, preferred_element_type=F32) for part in split(-(steps * decay)))
    both = jnp.concatenate(split(jnp.concatenate([steps, cumulative], axis=0)), axis=1)
    both = jnp.dot(both, pick_ref[...], preferred_element_type=F32)
    steps, cumulative = both[:length], both[length:]
    lane = lax.broadcasted_iota(jnp.int32, (length, width), 1) & (HEADDIM - 1)
    line = lax.broadcasted_iota(jnp.int32, (length, width), 0)
    own = lane == line
    cum_row = jnp.sum(jnp.where(own, cumulative, 0.0), axis=0, keepdims=True)
    step_row = jnp.sum(jnp.where(own, steps, 0.0), axis=0, keepdims=True)
    last = cumulative[length - 1 : length, :]
    causal = (token((length, width), 1, HEADDIM) <= token((length, width), 0, 64)) & (lane < length)
    mixing = jnp.exp(jnp.where(causal, cumulative - cum_row, -1e30)) * step_row
    half = lax.broadcasted_iota(jnp.int32, (length, 2 * HEADDIM), 1) < HEADDIM
    spare = jnp.zeros((HEADDIM - length, NSTATE), BF16)
    twice = jnp.concatenate([input_mix, spare, input_mix, spare], axis=0)
    scores = dot_nt(output_mix, twice)
    inputs16 = head_inputs.astype(BF16)
    inside = []
    for pair in range(heads // 2):
        low = pair * 2 * HEADDIM
        inputs = inputs16[:, low : low + 2 * HEADDIM]
        zero = jnp.zeros_like(inputs)
        pad = jnp.zeros((HEADDIM - length, 2 * HEADDIM), BF16)
        both = jnp.concatenate([jnp.where(half, inputs, zero), pad, jnp.where(half, zero, inputs), pad], axis=0)
        mix = (mixing[:, low : low + 2 * HEADDIM] * scores).astype(BF16)
        inside.append(jnp.dot(mix, both, preferred_element_type=F32))
    inside = jnp.concatenate(inside, axis=1)
    state = state_ref[0]
    carried = jnp.exp(cumulative) * dot_nt(output_mix, state)
    scanned = inside + carried + skip * head_inputs
    gated = scanned * (gate_inputs / (1.0 + jnp.exp(-gate_inputs)))
    channel = lax.broadcasted_iota(jnp.int32, (width, 128), 0)
    member = lax.broadcasted_iota(jnp.int32, (width, 128), 1) * group_width
    member = ((channel >= member) & (channel < member + group_width)).astype(BF16)
    squares = jnp.dot((gated * gated).astype(BF16), member, preferred_element_type=F32)
    scale = lax.rsqrt(squares * (1.0 / group_width) + 1e-05)
    position = lax.broadcasted_iota(jnp.int32, (length, width), 1)
    spread_scale = jnp.broadcast_to(scale[:, 0:1], (length, width))
    for group in range(1, width // group_width):
        spread_scale = jnp.where(position >= group * group_width, scale[:, group : group + 1], spread_scale)
    normed_ref[...] = (gated * spread_scale * gain).astype(BF16)
    to_end = (jnp.exp(last - cumulative) * steps * head_inputs).astype(BF16)
    added = lax.dot_general(to_end, input_mix, (((0,), (0,)), ((), ())), preferred_element_type=F32)
    head_rows = -(-heads // 8) * 8
    head_of = lax.broadcasted_iota(jnp.int32, (head_rows, width), 1)
    first = lax.broadcasted_iota(jnp.int32, (head_rows, width), 0) * HEADDIM
    whole = jnp.sum(jnp.where(head_of == first, last, 0.0), axis=1, keepdims=True)
    whole = jnp.broadcast_to(jnp.exp(whole), (head_rows, NSTATE))
    for head in range(heads):
        rows = slice(head * HEADDIM, (head + 1) * HEADDIM)
        carry_ref[0, rows, :] = state[rows].astype(F32) * whole[head : head + 1, :] + added[rows]


def scan(slots, total, state, rows, per_head, picked, carry, total_slots, group_width):
    count, width, _ = state.shape
    length = total.shape[0] // total_slots
    more = [] if carry is None else [pl.BlockSpec(memory_space=pl.ANY)]
    return pl.pallas_call(
        functools.partial(scan_kernel, width // HEADDIM, group_width),
        grid_spec=pltpu.PrefetchScalarGridSpec(
            num_scalar_prefetch=1,
            grid=(count,),
            in_specs=[
                pl.BlockSpec((length, total.shape[1]), lambda i, slots: (slots[i], 0)),
                pl.BlockSpec((1, width, NSTATE), lambda i, slots: (i, 0, 0)),
                pl.BlockSpec(rows.shape, lambda i, slots: (0, 0)),
                pl.BlockSpec(per_head.shape, lambda i, slots: (0, 0)),
                pl.BlockSpec(picked.shape, lambda i, slots: (0, 0)),
            ]
            + more,
            out_specs=(
                pl.BlockSpec((length, width), lambda i, slots: (i, 0)),
                pl.BlockSpec((1, width, NSTATE), lambda i, slots: (slots[i], 0, 0)),
            ),
        ),
        out_shape=(
            jax.ShapeDtypeStruct((count * length, width), BF16),
            jax.ShapeDtypeStruct((total_slots, width, NSTATE), F32),
        ),
        input_output_aliases={} if carry is None else {6: 1},
        compiler_params=params(),
        cost_estimate=cost(),
    )(slots, total, state, rows, per_head, picked, *(() if carry is None else (carry,)))


def terms_kernel(at_ref, normed_ref, dense_ref, out_ref):
    out_ref[0] = jnp.dot(normed_ref[...], dense_ref[0], preferred_element_type=F32).astype(BF16)


def terms(at, normed, dense, first, count):
    rows, depth = normed.shape
    shards, _, width = dense.shape
    return pl.pallas_call(
        terms_kernel,
        grid_spec=pltpu.PrefetchScalarGridSpec(
            num_scalar_prefetch=1,
            grid=(count,),
            in_specs=[
                pl.BlockSpec((rows, depth), lambda i, at: (0, 0)),
                pl.BlockSpec((1, depth, width), lambda i, at: (lax.rem(at[1] + 2 * shards - first - i, shards), 0, 0)),
            ],
            out_specs=pl.BlockSpec((1, rows, width), lambda i, at: (i, 0, 0)),
        ),
        out_shape=jax.ShapeDtypeStruct((count, rows, width), BF16),
        compiler_params=params(),
        cost_estimate=cost(),
    )(at, normed, dense)


def add(got, term):
    return (got.astype(F32) + term.astype(F32)).astype(BF16)


def place_kernel(slots_ref, got_ref, term_ref, *rest):
    out_ref = rest[-1]
    total = got_ref[...].astype(F32) + term_ref[0].astype(F32)
    patch, frames = out_ref.shape[1:3]
    for token in range(patch):
        out_ref[0, token] = total[token * frames : (token + 1) * frames].astype(BF16)


def place(slots, got, term, which, total_slots, before):
    rows, width = got.shape
    count = slots.shape[0]
    patch = rows // count // FRAMES
    return pl.pallas_call(
        place_kernel,
        grid_spec=pltpu.PrefetchScalarGridSpec(
            num_scalar_prefetch=1,
            grid=(count,),
            in_specs=[
                pl.BlockSpec((rows // count, width), lambda i, slots: (i, 0)),
                pl.BlockSpec((1, rows // count, width), lambda i, slots: (which, i, 0)),
            ]
            + ([] if before is None else [pl.BlockSpec(memory_space=pl.ANY)]),
            out_specs=pl.BlockSpec((1, patch, FRAMES, width), lambda i, slots: (slots[i], 0, 0, 0)),
        ),
        out_shape=jax.ShapeDtypeStruct((total_slots, patch, FRAMES, width), BF16),
        input_output_aliases={} if before is None else {3: 0},
        compiler_params=params(),
        cost_estimate=cost(),
    )(slots, got, term, *(() if before is None else (before,)))


def swap(value, bit, size):
    return lax.ppermute(value, "stream", [(i, i ^ bit) for i in range(size)])


def cube(own, size):
    return {0: [own], 2: [swap(own, 2, size)], 4: [swap(own, 4, size)]}


def cube_rest(got, size, near):
    half = got[0][0].shape[0] // 2
    got[6] = [swap(got[4][0][:half], 2, size), swap(got[2][0][half:], 4, size)]
    for bits in near:
        got[bits | 1] = [swap(part, 1, size) for part in got[bits]]
    return got


def after(values, earlier):
    return lax.optimization_barrier((values, earlier))[0]


def sparse(
    frames_in,
    kept_state,
    moved_to,
    xz_weight,
    side_weight,
    xz_mask,
    dt_bias,
    decay_rate,
    skip_gain,
    norm_gain,
    out_weight,
    out_mask,
):
    streams, shards = lax.axis_size("stream"), lax.axis_size("shard")
    me, shard = lax.axis_index("stream"), lax.axis_index("shard")
    slots, heads = kept_state.shape[:2]
    width = heads * HEADDIM
    block_rows = out_weight.shape[0] // BLOCK
    out_blocks = block_rows * (width // BLOCK)
    xz_room, out_room = int(2 * out_blocks * XZ_SHARE), int(out_blocks * OUT_SHARE)
    at = jnp.stack([me, shard]).astype(jnp.int32)

    frames = frames_in.transpose(0, 2, 1, 3).reshape(-1, frames_in.shape[3])
    features = lax.all_gather(frames, "shard", axis=1, tiled=True)

    side_blocks = -(-side_weight.shape[1] // BLOCK)
    xz_panel = after(xz_weight, frames).reshape(xz_weight.shape[0], -1)
    xz_packed = pack(at, xz_mask, xz_panel, 2, 0, xz_room, False, side_weight.T)
    xz_panels = cube(xz_packed, streams)

    steps = (1, 2, 3, streams // 2)
    match = (moved_to // slots - me) % streams == jnp.array(steps)[:, None]
    rank = jnp.cumsum(match.astype(jnp.int32), axis=1) - 1
    chosen = match[:, None, :] & (rank[:, None, :] == jnp.arange(MOST)[None, :, None])
    order = jnp.sum(jnp.where(chosen, jnp.arange(slots), 0), axis=2, dtype=jnp.int32)
    landing = jnp.sum(jnp.where(chosen, moved_to % slots, 0), axis=2, dtype=jnp.int32)

    def move(values, k):
        return lax.ppermute(values, "stream", [(i, (i + steps[k]) % streams) for i in range(streams)])

    landing = [move(after(landing, xz_packed)[k], k) for k in range(len(steps))]
    order = after(order, xz_packed)
    flat_state = kept_state.reshape(slots, width, NSTATE)
    sends = [pick(order[k], flat_state) for k in range(len(steps))]
    out_packed = pack(at, after(out_mask, xz_packed), out_weight, 1, 0, out_room, True)
    xz_table = slot_table(xz_mask, streams, shard, shards, side_blocks)
    out_table = slot_table(out_mask, streams, shard, shards, 0)
    head_of = jnp.arange(width) // HEADDIM
    picked = (shard * heads + head_of[None, :] == jnp.arange(BLOCK)[:, None]).astype(BF16)
    picked = jnp.concatenate([picked] * 3, axis=0)
    per_head = jnp.zeros((8, BLOCK), F32)
    per_head = lax.dynamic_update_slice(per_head, jnp.stack([dt_bias, decay_rate]), (0, shard * heads))
    rows = jnp.stack([jnp.repeat(skip_gain, HEADDIM), norm_gain] + [jnp.zeros_like(norm_gain)] * 6)

    xz_panels[2], xz_panels[4] = after(
        (xz_panels[2], xz_panels[4]), (sends, out_packed, xz_table, out_table, picked, per_head, rows, landing)
    )
    xz_panels = cube_rest(xz_panels, streams, (0, 2, 4, 6))

    sends[0], out_packed = after((sends[0], out_packed), xz_panels[6])
    got = [move(sends[0], 0)]
    out_panels = cube(out_packed, streams)
    masks = after((xz_mask, out_mask), (xz_panels[6], features))
    kept_xz, kept_out = (fullest(mask, streams, shards) for mask in masks)
    extra = (kept_xz > xz_room) | (kept_out > out_room)
    spare_xz, spare_out = 2 * out_blocks - xz_room, out_blocks - out_room

    def none(*_):
        return unwritten((streams, spare_xz, BLOCK, BLOCK)), unwritten((streams, spare_out, BLOCK, BLOCK))

    def some(xz_panel, out_weight):
        over_xz = pack(at, xz_mask, xz_panel, 2, xz_room, spare_xz, False)
        over_out = pack(at, out_mask, out_weight, 1, out_room, spare_out, True)
        return tuple(lax.all_gather(over, "stream", axis=0) for over in (over_xz, over_out))

    over_xz, over_out = lax.cond(extra, some, none, xz_panel, out_weight)
    at = jnp.concatenate([at, extra.astype(jnp.int32)[None]])
    total = project(after(at, got[0]), xz_table, features, xz_panels, over_xz, block_rows)
    out_panels[2], out_panels[4], total = lax.optimization_barrier((out_panels[2], out_panels[4], total))
    out_panels = cube_rest(out_panels, streams, (0, 2, 4))
    sends[1:] = after(sends[1:], out_panels[6])
    got += [move(sends[k], k) for k in range(1, len(steps))]

    pairs = streams // 2
    ring = [(i, (i + 1) % shards) for i in range(shards)]
    count = len(steps)

    def scan_chunk(k, total, carry):
        return scan(landing[k], total, got[k], rows, per_head, picked, carry, slots, DINNER // NORM_GROUPS)

    dense = expand(at, out_table, out_panels, over_out, 0, pairs - 1, block_rows, None)
    done, carry = scan_chunk(0, total, None)
    last = after(out_panels[2 * pairs - 2], (dense, done))
    out_panels[2 * pairs - 2] = last
    out_panels[2 * pairs - 1] = [swap(part, 1, streams) for part in last]
    dense = expand(at, out_table, out_panels, over_out, pairs - 1, 1, block_rows, dense)

    mixed, moving, term = None, [], []
    for step in range(count + shards - 1):
        if step < count:
            if step:
                done, carry = scan_chunk(step, total, carry)
            first = terms(at, done, dense, 1, 1)
            moving.append(lax.ppermute(first[0], "shard", ring))
            term.append(terms(at, after(done, first), dense, 2, shards - 1))
        passed = []
        for k in range(max(step - shards, 0), min(step, count)):
            hop = step - k + 1
            if hop < shards:
                passed.append(add(moving[k], term[k][hop - 2]))
                moving[k] = lax.ppermute(passed[-1], "shard", ring)
            elif hop == shards:
                mixed = place(landing[k], moving[k], term[k], shards - 2, slots, mixed)
        total = after(total, (term[-1], passed))
    return mixed.transpose(0, 2, 1, 3), carry.reshape(kept_state.shape)


def fullest(mask, panels, shards):
    rows = mask.reshape(panels, -1, mask.shape[-1])
    cells = rows.reshape(panels, rows.shape[1], shards, -1)
    return jnp.max(jnp.sum(cells, axis=(1, 3)))


def on_device(streams, shards, *args):
    xz_weight, out_weight, kept_state = args[3], args[10], args[1]
    rows, width = out_weight.shape
    regular = (
        streams == 8
        and streams % shards == 0
        and rows % BLOCK == 0
        and width % BLOCK == 0
        and width % (DINNER // NORM_GROUPS) == 0
        and width == (streams // shards) * rows
        and streams // shards == 2
        and args[9].shape[0] == width
        and kept_state.shape[1] % 2 == 0
    )
    if not regular:
        return general(*args)
    return sparse(*args)


def solution(mesh):
    placed = (
        P("stream", None, None, "shard"),
        P("stream", "shard", None, None),
        P("stream"),
        P("stream", None, "shard"),
        P("stream", None),
        P(),
        P("shard"),
        P("shard"),
        P("shard"),
        P("shard"),
        P("stream", "shard"),
        P(),
    )
    return jax.shard_map(
        functools.partial(on_device, mesh.shape["stream"], mesh.shape["shard"]),
        mesh=mesh,
        in_specs=placed,
        out_specs=(P("stream", None, None, "shard"), P("stream", "shard", None, None)),
        check_vma=False,
    )
```

```python
import functools

import jax
import jax.numpy as jnp
from jax import lax
from jax.experimental import pallas as pl
from jax.experimental.pallas import tpu as pltpu
from jax.sharding import PartitionSpec as P

NSTATE = 128
NORM_GROUPS = 16
BLOCK = 128
FRAMES = 4
MOST = 3
DINNER = 5120


def frame_step(head_inputs, input_mix, output_mix, step_sizes, decay_rate, skip_gain, carry_state):
    highest = lax.Precision.HIGHEST
    length = head_inputs.shape[1]
    decays = -decay_rate * step_sizes
    cumulative = jnp.cumsum(decays, axis=1)
    causal = (jnp.arange(length)[:, None] >= jnp.arange(length)[None, :])[None, :, :, None]
    between = cumulative[:, :, None, :] - cumulative[:, None, :, :]
    weights = jnp.where(causal, jnp.exp(jnp.where(causal, between, 0.0)), 0.0)
    scores = jnp.einsum("sln,smn->slm", output_mix, input_mix, precision=highest)
    mixing = scores[:, :, :, None] * weights * step_sizes[:, None, :, :]
    inside = jnp.einsum("slmh,smhp->slhp", mixing, head_inputs, precision=highest)
    carried = jnp.exp(cumulative)[:, :, :, None] * jnp.einsum(
        "sln,shpn->slhp", output_mix, carry_state, precision=highest
    )
    outputs = inside + carried + skip_gain[None, None, :, None] * head_inputs
    to_end = jnp.exp(cumulative[:, -1:, :] - cumulative) * step_sizes
    carry_state = jnp.exp(cumulative[:, -1, :])[:, :, None, None] * carry_state + jnp.einsum(
        "slh,slhp,sln->shpn", to_end, head_inputs, input_mix, precision=highest
    )
    return (outputs, carry_state)


def column_table(column_ids, block_total):
    return (jnp.arange(block_total)[:, None] == (column_ids // BLOCK)[None, :]).astype(jnp.float32)


def row_table(panel_rows, block_rows):
    row_ids = jnp.arange(panel_rows)
    return ((row_ids // BLOCK)[:, None] == jnp.arange(block_rows)[None, :]).astype(jnp.float32)


def general(
    frames_in,
    kept_state,
    moved_to,
    xz_weight,
    side_weight,
    xz_mask,
    dt_bias,
    decay_rate,
    skip_gain,
    norm_gain,
    out_weight,
    out_mask,
):
    device_count = lax.axis_size("stream")
    shard_pos = lax.axis_index("shard")
    slots = kept_state.shape[0]
    target_dev = moved_to // slots
    target_slot = moved_to % slots
    slot_ids = jnp.arange(slots)
    same_dest = (target_dev[:, None] == target_dev[None, :]) & (
        slot_ids[:, None] > slot_ids[None, :]
    )
    ranking = jnp.sum(same_dest.astype(jnp.int32), axis=1)
    position = target_dev * MOST + ranking
    send_states = (
        jnp.zeros((device_count * MOST,) + kept_state.shape[1:], jnp.float32)
        .at[position]
        .set(kept_state)
    )
    send_slots = jnp.full((device_count * MOST,), -1, jnp.int32).at[position].set(target_slot)
    got_states, got_slots = (
        lax.all_to_all(
            send_states.astype(jnp.bfloat16), "stream", split_axis=0, concat_axis=0, tiled=True
        ).astype(send_states.dtype),
        lax.all_to_all(send_slots, "stream", split_axis=0, concat_axis=0, tiled=True),
    )
    landing = jnp.where(got_slots >= 0, got_slots, slots)
    carry_state = jnp.zeros_like(kept_state).at[landing].set(got_states, mode="drop")
    patch_len = frames_in.shape[2]
    local_rows = frames_in.reshape(-1, frames_in.shape[3])
    features = lax.all_gather(local_rows, "shard", axis=1, tiled=True)
    row_count = features.shape[0]
    width_local = xz_weight.shape[2]
    block_rows = xz_mask.shape[0]
    column_ids = shard_pos * width_local + jnp.arange(width_local)
    col_onehot = column_table(column_ids, xz_mask.shape[2])
    xz_keep = jnp.einsum("rgc,cl->rgl", xz_mask.astype(jnp.float32), col_onehot).reshape(
        block_rows, 2 * width_local
    )
    out_keep = jnp.dot(out_mask.astype(jnp.float32), col_onehot)
    panel = lax.all_gather(xz_weight, "stream", axis=0, tiled=True)
    panel_rows = panel.shape[0]
    keep_mask = jnp.dot(row_table(panel_rows, block_rows), xz_keep).astype(jnp.bfloat16)
    masked = panel.reshape(panel_rows, 2 * width_local) * keep_mask
    columns = features
    xz_total = jnp.dot(columns, masked, preferred_element_type=jnp.float32)
    columns = features
    side_total = jnp.dot(
        columns,
        lax.all_gather(side_weight, "stream", axis=0, tiled=True),
        preferred_element_type=jnp.float32,
    )
    head_count = dt_bias.shape[0]
    head_size = width_local // head_count
    head_inputs = xz_total[:, :width_local].reshape(slots, FRAMES, patch_len, head_count, head_size)
    gate_inputs = xz_total[:, width_local:]
    input_mix = side_total[:, :NSTATE].reshape(slots, FRAMES, patch_len, NSTATE)
    output_mix = side_total[:, NSTATE : 2 * NSTATE].reshape(slots, FRAMES, patch_len, NSTATE)
    step_raw = lax.dynamic_slice_in_dim(
        side_total, 2 * NSTATE + shard_pos * head_count, head_count, 1
    )
    step_sizes = jax.nn.softplus(step_raw + dt_bias).reshape(slots, FRAMES, patch_len, head_count)
    results = []
    for frame_index in range(FRAMES):
        outputs, carry_state = frame_step(
            head_inputs[:, frame_index],
            input_mix[:, frame_index],
            output_mix[:, frame_index],
            step_sizes[:, frame_index],
            decay_rate,
            skip_gain,
            carry_state,
        )
        results.append(outputs)
    scanned = jnp.stack(results, axis=1).reshape(row_count, width_local)
    gated = (scanned * jax.nn.silu(gate_inputs)).reshape(row_count, -1, DINNER // NORM_GROUPS)
    mean_square = jnp.mean(gated * gated, axis=2, keepdims=True)
    normed = (
        (gated * lax.rsqrt(mean_square + 1e-05)).reshape(row_count, width_local) * norm_gain
    ).astype(jnp.bfloat16)
    panel = lax.all_gather(out_weight, "stream", axis=0, tiled=True)
    panel_rows = panel.shape[0]
    keep_mask = jnp.dot(row_table(panel_rows, block_rows), out_keep).astype(jnp.bfloat16)
    partial_out = lax.dot_general(
        normed, panel * keep_mask, (((1,), (1,)), ((), ())), preferred_element_type=jnp.float32
    )
    mixed = lax.psum_scatter(
        partial_out.astype(jnp.bfloat16), "shard", scatter_dimension=1, tiled=True
    )
    return (mixed.reshape(slots, FRAMES, patch_len, -1), carry_state)


HEADDIM = 64
XZ_SHARE = 0.66
OUT_SHARE = 0.72
BF16 = jnp.bfloat16
F32 = jnp.float32
MIB = 1 << 20


def params(limit=48 * MIB):
    return pltpu.CompilerParams(vmem_limit_bytes=limit)


def cost():
    return pl.CostEstimate(flops=1, bytes_accessed=1, transcendentals=0)


def dot_nt(left, right):
    return lax.dot_general(left, right, (((1,), (1,)), ((), ())), preferred_element_type=F32)


def pack_kernel(block_rows, groups, columns, mask_columns, low_count, room, always, turn, at_ref, mask_ref, x_ref, *rest):
    out_ref = rest[-1]
    panel, shard = at_ref[0], at_ref[1]
    base = 0
    if low_count == 0:
        base = 1 + block_rows * always
        out_ref[0] = jnp.zeros((BLOCK, BLOCK), BF16)
        for row in range(block_rows):
            for column in range(always):
                block = rest[0][column * BLOCK : (column + 1) * BLOCK, row * BLOCK : (row + 1) * BLOCK].T
                short = BLOCK - block.shape[1]
                if short:
                    block = jnp.concatenate([block, jnp.zeros((BLOCK, short), BF16)], axis=1)
                out_ref[1 + row * always + column] = block
    count = jnp.int32(-low_count)
    for row in range(block_rows):
        for group in range(groups):
            for column in range(columns):
                place = ((panel * block_rows + row) * groups + group) * mask_columns + shard * columns + column
                keep = mask_ref[place] != 0
                low = (group * columns + column) * BLOCK

                @pl.when(keep & (count >= 0) & (count < room))
                def _(count=count, low=low, row=row):
                    block = x_ref[row * BLOCK : (row + 1) * BLOCK, low : low + BLOCK]
                    out_ref[base + count] = block.T if turn else block

                count = count + keep.astype(jnp.int32)


def pack(at, mask, panel, groups, low_count, room, turn, beside=None):
    rows, width = panel.shape
    columns = width // groups // BLOCK
    always = 0 if beside is None else -(-beside.shape[0] // BLOCK)
    smem = pl.BlockSpec(memory_space=pltpu.SMEM)
    vmem = pl.BlockSpec(memory_space=pltpu.VMEM)
    extra = () if beside is None else (beside,)
    size = room if low_count else 1 + rows // BLOCK * always + room
    return pl.pallas_call(
        functools.partial(
            pack_kernel, rows // BLOCK, groups, columns, mask.shape[-1], low_count, room, always, turn
        ),
        out_shape=jax.ShapeDtypeStruct((size, BLOCK, BLOCK), BF16),
        in_specs=[smem, smem, vmem] + [vmem] * len(extra),
        out_specs=vmem,
        compiler_params=params(),
        cost_estimate=cost(),
    )(at, mask.reshape(-1), panel, *extra)


def unwritten(shape):
    return pl.pallas_call(
        lambda out_ref: None,
        out_shape=jax.ShapeDtypeStruct(shape, BF16),
        out_specs=pl.BlockSpec(memory_space=pl.ANY),
        cost_estimate=cost(),
    )()


def slot_table(mask, panels, shard, shards, always):
    rows = mask.shape[0] // panels
    mine = lax.dynamic_slice_in_dim(mask, shard * (mask.shape[-1] // shards), mask.shape[-1] // shards, mask.ndim - 1)
    kept = mine.reshape(panels, -1)
    size = kept.shape[1]
    before = (jnp.arange(size)[:, None] < jnp.arange(size)[None, :]).astype(F32)
    rank = jnp.dot(kept.astype(F32), before).astype(jnp.int32)
    table = jnp.where(kept != 0, rank + 1 + rows * always, 0).reshape(panels, rows, -1)
    fixed = 1 + jnp.arange(rows)[:, None] * always + jnp.arange(always)[None, :]
    fixed = jnp.broadcast_to(fixed[None], (panels, rows, always)).astype(jnp.int32)
    return jnp.concatenate([table, fixed], axis=2).reshape(-1)


def panel_copies(parts, over, panel, held, sems):
    copies, low = [], 0
    for i, part in enumerate(parts):
        copies.append(pltpu.make_async_copy(part, held.at[pl.ds(low, part.shape[0])], sems.at[i]))
        low += part.shape[0]
    return copies, pltpu.make_async_copy(over.at[panel], held.at[pl.ds(low, over.shape[1])], sems.at[2])


def project_kernel(counts, block_rows, blocks, tiles, at_ref, table_ref, x_ref, over_ref, *refs):
    out_ref, held, x_held, *dense, total, sems, x_sems, out_sems = refs[len(refs) - 9 :]
    parts, low = [], 0
    for count in counts:
        parts.append(refs[low : low + count])
        low += count
    me, extra = at_ref[0], at_ref[2] != 0
    depth = block_rows * BLOCK
    pairs = len(counts) // 2

    def fetch(pair):
        slot, plain, more = pair % 2, [], []
        for side in range(2):
            panel = me ^ (2 * pair + side)
            copies, over = panel_copies(
                parts[2 * pair + side], over_ref, panel, held.at[slot, side], sems.at[slot, side]
            )
            columns = pl.ds(pl.multiple_of(panel * depth, BLOCK), depth)
            copies.append(
                pltpu.make_async_copy(
                    x_ref.at[:, columns], x_held.at[slot, :, pl.ds(side * depth, depth)], x_sems.at[slot, side]
                )
            )
            plain += copies
            more.append(over)
        return plain, more

    def start(pair):
        plain, more = fetch(pair)
        for copy in plain:
            copy.start()

        @pl.when(extra)
        def _():
            for copy in more:
                copy.start()

    def wait(pair):
        plain, more = fetch(pair)
        for copy in plain:
            copy.wait()

        @pl.when(extra)
        def _():
            for copy in more:
                copy.wait()

    def out_copy(n):
        first, size = tiles[n]
        columns = pl.ds(first * BLOCK, size * BLOCK)
        return pltpu.make_async_copy(total.at[:, columns], out_ref.at[:, columns], out_sems.at[n])

    def fill(pair, n):
        first, size = tiles[n]
        for side in range(2):
            panel = me ^ (2 * pair + side)
            for row in range(block_rows):
                line = (panel * block_rows + row) * blocks + first
                high = (side * block_rows + row) * BLOCK
                for column in range(size):
                    dense[n % 2][high : high + BLOCK, column * BLOCK : (column + 1) * BLOCK] = held[
                        pair % 2, side, table_ref[line + column]
                    ]

    def multiply(pair, n):
        first, size = tiles[n]
        columns = slice(first * BLOCK, (first + size) * BLOCK)
        term = jnp.dot(x_held[pair % 2], dense[n % 2][:, : size * BLOCK], preferred_element_type=F32)
        total[:, columns] = term + jnp.where(pair > 0, total[:, columns], 0.0)

    start(0)

    @pl.loop(0, pairs)
    def _(pair):
        for i in range(pairs):

            @pl.when(pair == i)
            def _(i=i):
                wait(i)
                if i + 1 < pairs:
                    start(i + 1)

        fill(pair, 0)
        for n in range(len(tiles)):
            if n + 1 < len(tiles):
                fill(pair, n + 1)
            multiply(pair, n)

            @pl.when(pair == pairs - 1)
            def _(n=n):
                out_copy(n).start()

    for n in range(len(tiles)):
        out_copy(n).wait()


def project(at, table, features, panels, over, block_rows, wide=4):
    rows = features.shape[0]
    count = len(panels)
    blocks = table.shape[0] // (count * block_rows)
    size = sum(part.shape[0] for part in panels[0]) + over.shape[1]
    flat = [part for bits in range(count) for part in panels[bits]]
    smem = pl.BlockSpec(memory_space=pltpu.SMEM)
    anywhere = pl.BlockSpec(memory_space=pl.ANY)
    depth = 2 * block_rows * BLOCK
    tiles = [(first, min(wide, blocks - first)) for first in range(0, blocks, wide)]
    return pl.pallas_call(
        functools.partial(project_kernel, [len(panels[b]) for b in range(count)], block_rows, blocks, tiles),
        out_shape=jax.ShapeDtypeStruct((rows, blocks * BLOCK), F32),
        in_specs=[smem, smem] + [anywhere] * (2 + len(flat)),
        out_specs=anywhere,
        scratch_shapes=[
            pltpu.VMEM((2, 2, size, BLOCK, BLOCK), BF16),
            pltpu.VMEM((2, rows, depth), BF16),
            pltpu.VMEM((depth, wide * BLOCK), BF16),
            pltpu.VMEM((depth, wide * BLOCK), BF16),
            pltpu.VMEM((rows, blocks * BLOCK), F32),
            pltpu.SemaphoreType.DMA((2, 2, 3)),
            pltpu.SemaphoreType.DMA((2, 2)),
            pltpu.SemaphoreType.DMA((len(tiles),)),
        ],
        compiler_params=params(56 * MIB),
        cost_estimate=cost(),
    )(at, table, features, over, *flat)


def pick_kernel(order_ref, x_ref, out_ref):
    out_ref[...] = x_ref[...].astype(out_ref.dtype)


def pick(order, states):
    count, block = order.shape[0], (1,) + states.shape[1:]
    return pl.pallas_call(
        pick_kernel,
        grid_spec=pltpu.PrefetchScalarGridSpec(
            num_scalar_prefetch=1,
            grid=(count,),
            in_specs=[pl.BlockSpec(block, lambda i, order: (order[i], 0, 0))],
            out_specs=pl.BlockSpec(block, lambda i, order: (i, 0, 0)),
        ),
        out_shape=jax.ShapeDtypeStruct((count,) + states.shape[1:], BF16),
        compiler_params=params(),
        cost_estimate=cost(),
    )(order, states)


def split(values):
    high = values.astype(BF16)
    left = values - high.astype(F32)
    middle = left.astype(BF16)
    return high, middle, (left - middle.astype(F32)).astype(BF16)


def scan_kernel(heads, group_width, slots_ref, total_ref, state_ref, rows_ref, heads_ref, pick_ref, *rest):
    normed_ref, carry_ref = rest[-2:]
    length, width = normed_ref.shape
    head_inputs = total_ref[:, :width]
    gate_inputs = total_ref[:, width : 2 * width]
    side = 2 * width
    input_mix = total_ref[:, side : side + NSTATE].astype(BF16)
    output_mix = total_ref[:, side + NSTATE : side + 2 * NSTATE].astype(BF16)
    bias, decay = heads_ref[0:1, :], heads_ref[1:2, :]
    skip, gain = rows_ref[0:1, :], rows_ref[1:2, :]
    raw = total_ref[:, side + 2 * NSTATE : side + 2 * NSTATE + heads_ref.shape[1]] + bias
    steps = jnp.maximum(raw, 0.0) + jnp.log1p(jnp.exp(-jnp.abs(raw)))
    patch = length // FRAMES

    def token(shape, axis, size):
        row = lax.broadcasted_iota(jnp.int32, shape, axis) & (size - 1)
        return (row & (FRAMES - 1)) * patch + row // FRAMES

    square = (length, length)
    lower = (token(square, 0, 64) >= token(square, 1, 64)).astype(BF16)
    cumulative = sum(jnp.dot(lower, part, preferred_element_type=F32) for part in split(-(steps * decay)))
    both = jnp.concatenate(split(jnp.concatenate([steps, cumulative], axis=0)), axis=1)
    both = jnp.dot(both, pick_ref[...], preferred_element_type=F32)
    steps, cumulative = both[:length], both[length:]
    lane = lax.broadcasted_iota(jnp.int32, (length, width), 1) & (HEADDIM - 1)
    line = lax.broadcasted_iota(jnp.int32, (length, width), 0)
    own = lane == line
    cum_row = jnp.sum(jnp.where(own, cumulative, 0.0), axis=0, keepdims=True)
    step_row = jnp.sum(jnp.where(own, steps, 0.0), axis=0, keepdims=True)
    last = cumulative[length - 1 : length, :]
    causal = (token((length, width), 1, HEADDIM) <= token((length, width), 0, 64)) & (lane < length)
    mixing = jnp.exp(jnp.where(causal, cumulative - cum_row, -1e30)) * step_row
    half = lax.broadcasted_iota(jnp.int32, (length, 2 * HEADDIM), 1) < HEADDIM
    spare = jnp.zeros((HEADDIM - length, NSTATE), BF16)
    twice = jnp.concatenate([input_mix, spare, input_mix, spare], axis=0)
    scores = dot_nt(output_mix, twice)
    inputs16 = head_inputs.astype(BF16)
    inside = []
    for pair in range(heads // 2):
        low = pair * 2 * HEADDIM
        inputs = inputs16[:, low : low + 2 * HEADDIM]
        zero = jnp.zeros_like(inputs)
        pad = jnp.zeros((HEADDIM - length, 2 * HEADDIM), BF16)
        both = jnp.concatenate([jnp.where(half, inputs, zero), pad, jnp.where(half, zero, inputs), pad], axis=0)
        mix = (mixing[:, low : low + 2 * HEADDIM] * scores).astype(BF16)
        inside.append(jnp.dot(mix, both, preferred_element_type=F32))
    inside = jnp.concatenate(inside, axis=1)
    state = state_ref[0]
    carried = jnp.exp(cumulative) * dot_nt(output_mix, state)
    scanned = inside + carried + skip * head_inputs
    gated = scanned * (gate_inputs / (1.0 + jnp.exp(-gate_inputs)))
    channel = lax.broadcasted_iota(jnp.int32, (width, 128), 0)
    member = lax.broadcasted_iota(jnp.int32, (width, 128), 1) * group_width
    member = ((channel >= member) & (channel < member + group_width)).astype(BF16)
    squares = jnp.dot((gated * gated).astype(BF16), member, preferred_element_type=F32)
    scale = lax.rsqrt(squares * (1.0 / group_width) + 1e-05)
    position = lax.broadcasted_iota(jnp.int32, (length, width), 1)
    spread_scale = jnp.broadcast_to(scale[:, 0:1], (length, width))
    for group in range(1, width // group_width):
        spread_scale = jnp.where(position >= group * group_width, scale[:, group : group + 1], spread_scale)
    normed_ref[...] = (gated * spread_scale * gain).astype(BF16)
    to_end = (jnp.exp(last - cumulative) * steps * head_inputs).astype(BF16)
    added = lax.dot_general(to_end, input_mix, (((0,), (0,)), ((), ())), preferred_element_type=F32)
    head_rows = -(-heads // 8) * 8
    head_of = lax.broadcasted_iota(jnp.int32, (head_rows, width), 1)
    first = lax.broadcasted_iota(jnp.int32, (head_rows, width), 0) * HEADDIM
    whole = jnp.sum(jnp.where(head_of == first, last, 0.0), axis=1, keepdims=True)
    whole = jnp.broadcast_to(jnp.exp(whole), (head_rows, NSTATE))
    for head in range(heads):
        rows = slice(head * HEADDIM, (head + 1) * HEADDIM)
        carry_ref[0, rows, :] = state[rows].astype(F32) * whole[head : head + 1, :] + added[rows]


def scan(slots, total, state, rows, per_head, picked, carry, total_slots, group_width):
    count, width, _ = state.shape
    length = total.shape[0] // total_slots
    more = [] if carry is None else [pl.BlockSpec(memory_space=pl.ANY)]
    return pl.pallas_call(
        functools.partial(scan_kernel, width // HEADDIM, group_width),
        grid_spec=pltpu.PrefetchScalarGridSpec(
            num_scalar_prefetch=1,
            grid=(count,),
            in_specs=[
                pl.BlockSpec((length, total.shape[1]), lambda i, slots: (slots[i], 0)),
                pl.BlockSpec((1, width, NSTATE), lambda i, slots: (i, 0, 0)),
                pl.BlockSpec(rows.shape, lambda i, slots: (0, 0)),
                pl.BlockSpec(per_head.shape, lambda i, slots: (0, 0)),
                pl.BlockSpec(picked.shape, lambda i, slots: (0, 0)),
            ]
            + more,
            out_specs=(
                pl.BlockSpec((length, width), lambda i, slots: (i, 0)),
                pl.BlockSpec((1, width, NSTATE), lambda i, slots: (slots[i], 0, 0)),
            ),
        ),
        out_shape=(
            jax.ShapeDtypeStruct((count * length, width), BF16),
            jax.ShapeDtypeStruct((total_slots, width, NSTATE), F32),
        ),
        input_output_aliases={} if carry is None else {6: 1},
        compiler_params=params(),
        cost_estimate=cost(),
    )(slots, total, state, rows, per_head, picked, *(() if carry is None else (carry,)))


def expand_terms_kernel(counts, block_rows, blocks, first_pair, at_ref, table_ref, normed_ref, over_ref, *refs):
    term_ref, dense_ref, held, sems = refs[len(refs) - 4 :]
    me, extra = at_ref[0], at_ref[2] != 0
    pairs = len(counts) // 2
    step = pl.program_id(0)

    def each(number, act):
        slot = number % 2
        for pair in range(pairs):
            low = sum(counts[: 2 * pair])

            @pl.when(number == pair)
            def _(pair=pair, low=low):
                for side in range(2):
                    parts = refs[low : low + counts[2 * pair + side]]
                    low += counts[2 * pair + side]
                    panel = me ^ (2 * (first_pair + pair) + side)
                    plain, over = panel_copies(parts, over_ref, panel, held.at[slot, side], sems.at[slot, side])
                    for copy in plain:
                        act(copy)

                    @pl.when(extra)
                    def _(over=over):
                        act(over)

    @pl.when(step == 0)
    def _():
        each(0, lambda copy: copy.start())

    @pl.when(step + 1 < pairs)
    def _():
        each(step + 1, lambda copy: copy.start())

    each(step, lambda copy: copy.wait())
    for side in range(2):
        panel = me ^ (2 * (first_pair + step) + side)
        place = (panel % 2) * (block_rows * BLOCK)
        for row in range(block_rows):
            columns = pl.ds(pl.multiple_of(place + row * BLOCK, BLOCK), BLOCK)
            line = (panel * block_rows + row) * blocks
            for column in range(blocks):
                dense_ref[0, column * BLOCK : (column + 1) * BLOCK, columns] = held[
                    step % 2, side, table_ref[line + column]
                ]
    term_ref[...] = jnp.dot(normed_ref[...], dense_ref[0], preferred_element_type=F32).astype(BF16)


def expand_terms(at, table, normed, panels, over, first_pair, pairs, block_rows, before):
    rows, depth = normed.shape
    count = over.shape[0]
    blocks = table.shape[0] // (count * block_rows)
    chosen = [panels[2 * first_pair + i] for i in range(2 * pairs)]
    flat = [part for parts in chosen for part in parts]
    size = sum(part.shape[0] for part in chosen[0]) + over.shape[1]
    anywhere = pl.BlockSpec(memory_space=pl.ANY)
    width = 2 * block_rows * BLOCK
    more = [] if before is None else list(before)

    def dest(i, at):
        return (at[0] // 2) ^ (first_pair + i)

    return pl.pallas_call(
        functools.partial(expand_terms_kernel, [len(parts) for parts in chosen], block_rows, blocks, first_pair),
        grid_spec=pltpu.PrefetchScalarGridSpec(
            num_scalar_prefetch=2,
            grid=(pairs,),
            in_specs=[pl.BlockSpec((rows, depth), lambda i, at, table: (0, 0))]
            + [anywhere] * (1 + len(flat) + len(more)),
            out_specs=(
                pl.BlockSpec((rows, width), lambda i, at, table: (0, dest(i, at))),
                pl.BlockSpec((1, depth, width), lambda i, at, table: (dest(i, at), 0, 0)),
            ),
            scratch_shapes=[
                pltpu.VMEM((2, 2, size, BLOCK, BLOCK), BF16),
                pltpu.SemaphoreType.DMA((2, 2, 3)),
            ],
        ),
        out_shape=(
            jax.ShapeDtypeStruct((rows, count // 2 * width), BF16),
            jax.ShapeDtypeStruct((count // 2, depth, width), BF16),
        ),
        input_output_aliases={4 + len(flat): 0, 5 + len(flat): 1} if more else {},
        compiler_params=params(),
        cost_estimate=cost(),
    )(at, table, normed, over, *flat, *more)


def terms_kernel(normed_ref, dense_ref, out_ref):
    out_ref[...] = jnp.dot(normed_ref[...], dense_ref[0], preferred_element_type=F32).astype(BF16)


def terms(normed, dense):
    rows, depth = normed.shape
    shards, _, width = dense.shape
    return pl.pallas_call(
        terms_kernel,
        grid=(shards,),
        in_specs=[
            pl.BlockSpec((rows, depth), lambda i: (0, 0)),
            pl.BlockSpec((1, depth, width), lambda i: (i, 0, 0)),
        ],
        out_specs=pl.BlockSpec((rows, width), lambda i: (0, i)),
        out_shape=jax.ShapeDtypeStruct((rows, shards * width), BF16),
        compiler_params=params(),
        cost_estimate=cost(),
    )(normed, dense)


def add(got, term):
    return (got.astype(F32) + term.astype(F32)).astype(BF16)


def place_kernel(slots_ref, got_ref, *rest):
    out_ref = rest[-1]
    total = got_ref[...].astype(F32)
    patch, frames = out_ref.shape[1:3]
    for token in range(patch):
        out_ref[0, token] = total[token * frames : (token + 1) * frames].astype(BF16)


def place(slots, got, total_slots, before):
    rows, width = got.shape
    count = slots.shape[0]
    patch = rows // count // FRAMES
    return pl.pallas_call(
        place_kernel,
        grid_spec=pltpu.PrefetchScalarGridSpec(
            num_scalar_prefetch=1,
            grid=(count,),
            in_specs=[pl.BlockSpec((rows // count, width), lambda i, slots: (i, 0))]
            + ([] if before is None else [pl.BlockSpec(memory_space=pl.ANY)]),
            out_specs=pl.BlockSpec((1, patch, FRAMES, width), lambda i, slots: (slots[i], 0, 0, 0)),
        ),
        out_shape=jax.ShapeDtypeStruct((total_slots, patch, FRAMES, width), BF16),
        input_output_aliases={} if before is None else {2: 0},
        compiler_params=params(),
        cost_estimate=cost(),
    )(slots, got, *(() if before is None else (before,)))


def swap(value, bit, size):
    return lax.ppermute(value, "stream", [(i, i ^ bit) for i in range(size)])


def cube(own, size):
    return {0: [own], 2: [swap(own, 2, size)], 4: [swap(own, 4, size)], 1: [swap(own, 1, size)]}


def cube_rest(got, size, near):
    half = got[0][0].shape[0] // 2
    got[6] = [swap(got[4][0][:half], 2, size), swap(got[2][0][half:], 4, size)]
    for bits in near:
        got[bits | 1] = [swap(part, 1, size) for part in got[bits]]
    return got


def after(values, earlier):
    return lax.optimization_barrier((values, earlier))[0]


def sparse(
    frames_in,
    kept_state,
    moved_to,
    xz_weight,
    side_weight,
    xz_mask,
    dt_bias,
    decay_rate,
    skip_gain,
    norm_gain,
    out_weight,
    out_mask,
):
    streams, shards = lax.axis_size("stream"), lax.axis_size("shard")
    me, shard = lax.axis_index("stream"), lax.axis_index("shard")
    slots, heads = kept_state.shape[:2]
    width = heads * HEADDIM
    block_rows = out_weight.shape[0] // BLOCK
    out_blocks = block_rows * (width // BLOCK)
    xz_room, out_room = int(2 * out_blocks * XZ_SHARE), int(out_blocks * OUT_SHARE)
    at = jnp.stack([me, shard]).astype(jnp.int32)

    frames = frames_in.transpose(0, 2, 1, 3).reshape(-1, frames_in.shape[3])
    features = lax.all_gather(frames, "shard", axis=1, tiled=True)

    side_blocks = -(-side_weight.shape[1] // BLOCK)
    xz_panel = after(xz_weight, frames).reshape(xz_weight.shape[0], -1)
    xz_packed = pack(at, xz_mask, xz_panel, 2, 0, xz_room, False, side_weight.T)
    xz_panels = cube(xz_packed, streams)

    steps = (1, 2, 3, streams // 2)
    match = (moved_to // slots - me) % streams == jnp.array(steps)[:, None]
    rank = jnp.cumsum(match.astype(jnp.int32), axis=1) - 1
    chosen = match[:, None, :] & (rank[:, None, :] == jnp.arange(MOST)[None, :, None])
    order = jnp.sum(jnp.where(chosen, jnp.arange(slots), 0), axis=2, dtype=jnp.int32)
    landing = jnp.sum(jnp.where(chosen, moved_to % slots, 0), axis=2, dtype=jnp.int32)

    def move(values, k):
        return lax.ppermute(values, "stream", [(i, (i + steps[k]) % streams) for i in range(streams)])

    landing = [move(after(landing, xz_packed)[k], k) for k in range(len(steps))]
    order = after(order, xz_packed)
    flat_state = kept_state.reshape(slots, width, NSTATE)
    sends = [pick(order[k], flat_state) for k in range(len(steps))]
    out_packed = pack(at, after(out_mask, xz_packed), out_weight, 1, 0, out_room, True)
    masks = after((xz_mask, out_mask), sends)
    kept_xz, kept_out = (fullest(mask, streams, shards) for mask in masks)
    xz_table = slot_table(xz_mask, streams, shard, shards, side_blocks)
    out_table = slot_table(out_mask, streams, shard, shards, 0)
    head_of = jnp.arange(width) // HEADDIM
    picked = (shard * heads + head_of[None, :] == jnp.arange(BLOCK)[:, None]).astype(BF16)
    picked = jnp.concatenate([picked] * 3, axis=0)
    per_head = jnp.zeros((8, BLOCK), F32)
    per_head = lax.dynamic_update_slice(per_head, jnp.stack([dt_bias, decay_rate]), (0, shard * heads))
    rows = jnp.stack([jnp.repeat(skip_gain, HEADDIM), norm_gain] + [jnp.zeros_like(norm_gain)] * 6)

    (xz_panels[2], xz_panels[4], sends[0]) = after(
        (xz_panels[2], xz_panels[4], sends[0]), (xz_panels[1], sends, out_packed, kept_xz, kept_out, xz_table, out_table, picked, per_head, rows, landing)
    )
    got = [move(sends[0], 0)]
    xz_panels = cube_rest(xz_panels, streams, (2, 4, 6))

    out_packed = after(out_packed, (xz_panels[6], got))
    out_panels = cube(out_packed, streams)
    extra = after((kept_xz > xz_room) | (kept_out > out_room), (xz_panels[6], features))
    spare_xz, spare_out = 2 * out_blocks - xz_room, out_blocks - out_room

    def none(*_):
        return unwritten((streams, spare_xz, BLOCK, BLOCK)), unwritten((streams, spare_out, BLOCK, BLOCK))

    def some(xz_panel, out_weight):
        over_xz = pack(at, xz_mask, xz_panel, 2, xz_room, spare_xz, False)
        over_out = pack(at, out_mask, out_weight, 1, out_room, spare_out, True)
        return tuple(lax.all_gather(over, "stream", axis=0) for over in (over_xz, over_out))

    over_xz, over_out = lax.cond(extra, some, none, xz_panel, out_weight)
    at = jnp.concatenate([at, extra.astype(jnp.int32)[None]])
    total = project(at, xz_table, features, xz_panels, over_xz, block_rows)
    out_panels, total = lax.optimization_barrier((out_panels, total))
    out_panels = cube_rest(out_panels, streams, (2, 4))
    sends[1:] = after(sends[1:], out_panels[6])
    got.append(move(sends[1], 1))
    got += [move(sends[k], k) for k in range(2, len(steps))]

    pairs = streams // 2
    count = len(steps)

    def scan_chunk(k, total, carry):
        return scan(landing[k], total, got[k], rows, per_head, picked, carry, slots, DINNER // NORM_GROUPS)

    done, carry = scan_chunk(0, total, None)
    most = expand_terms(at, out_table, done, out_panels, over_out, 0, pairs - 1, block_rows, None)
    last = after(out_panels[2 * pairs - 2], most)
    out_panels[2 * pairs - 2] = last
    out_panels[2 * pairs - 1] = [swap(part, 1, streams) for part in last]
    term, dense = expand_terms(at, out_table, done, out_panels, over_out, pairs - 1, 1, block_rows, most)

    ring = [(i, (i + 1) % shards) for i in range(shards)]

    def term_for(k, hop):
        return lax.dynamic_slice_in_dim(terms_of[k], (shard - hop) % shards * width, width, 1)

    mixed, moving, terms_of = None, [], [term]
    for step in range(count + shards - 1):
        if step < count:
            if step:
                done, carry = scan_chunk(step, total, carry)
                terms_of.append(terms(done, dense))
            moving.append(lax.ppermute(term_for(step, 1), "shard", ring))
        passed = []
        for k in range(max(step - shards + 1, 0), min(step, count)):
            hop = step - k + 1
            value = add(moving[k], term_for(k, hop))
            passed.append(value)
            if hop < shards:
                moving[k] = lax.ppermute(value, "shard", ring)
            else:
                mixed = place(landing[k], value, slots, mixed)
        total = after(total, (terms_of[-1], passed))
    return mixed.transpose(0, 2, 1, 3), carry.reshape(kept_state.shape)


def fullest(mask, panels, shards):
    rows = mask.reshape(panels, -1, mask.shape[-1])
    cells = rows.reshape(panels, rows.shape[1], shards, -1)
    return jnp.max(jnp.sum(cells, axis=(1, 3)))


def on_device(streams, shards, *args):
    xz_weight, out_weight, kept_state = args[3], args[10], args[1]
    rows, width = out_weight.shape
    regular = (
        streams == 8
        and streams % shards == 0
        and rows % BLOCK == 0
        and width % BLOCK == 0
        and width % (DINNER // NORM_GROUPS) == 0
        and width == (streams // shards) * rows
        and streams // shards == 2
        and args[9].shape[0] == width
        and kept_state.shape[1] % 2 == 0
    )
    if not regular:
        return general(*args)
    return sparse(*args)


def solution(mesh):
    placed = (
        P("stream", None, None, "shard"),
        P("stream", "shard", None, None),
        P("stream"),
        P("stream", None, "shard"),
        P("stream", None),
        P(),
        P("shard"),
        P("shard"),
        P("shard"),
        P("shard"),
        P("stream", "shard"),
        P(),
    )
    return jax.shard_map(
        functools.partial(on_device, mesh.shape["stream"], mesh.shape["shard"]),
        mesh=mesh,
        in_specs=placed,
        out_specs=(P("stream", None, None, "shard"), P("stream", "shard", None, None)),
        check_vma=False,
    )
```

```python
import functools

import jax
import jax.numpy as jnp
from jax import lax
from jax.experimental import pallas as pl
from jax.experimental.pallas import tpu as pltpu
from jax.sharding import PartitionSpec as P

NSTATE = 128
NORM_GROUPS = 16
BLOCK = 128
FRAMES = 4
MOST = 3
DINNER = 5120


def frame_step(head_inputs, input_mix, output_mix, step_sizes, decay_rate, skip_gain, carry_state):
    highest = lax.Precision.HIGHEST
    length = head_inputs.shape[1]
    decays = -decay_rate * step_sizes
    cumulative = jnp.cumsum(decays, axis=1)
    causal = (jnp.arange(length)[:, None] >= jnp.arange(length)[None, :])[None, :, :, None]
    between = cumulative[:, :, None, :] - cumulative[:, None, :, :]
    weights = jnp.where(causal, jnp.exp(jnp.where(causal, between, 0.0)), 0.0)
    scores = jnp.einsum("sln,smn->slm", output_mix, input_mix, precision=highest)
    mixing = scores[:, :, :, None] * weights * step_sizes[:, None, :, :]
    inside = jnp.einsum("slmh,smhp->slhp", mixing, head_inputs, precision=highest)
    carried = jnp.exp(cumulative)[:, :, :, None] * jnp.einsum(
        "sln,shpn->slhp", output_mix, carry_state, precision=highest
    )
    outputs = inside + carried + skip_gain[None, None, :, None] * head_inputs
    to_end = jnp.exp(cumulative[:, -1:, :] - cumulative) * step_sizes
    carry_state = jnp.exp(cumulative[:, -1, :])[:, :, None, None] * carry_state + jnp.einsum(
        "slh,slhp,sln->shpn", to_end, head_inputs, input_mix, precision=highest
    )
    return (outputs, carry_state)


def column_table(column_ids, block_total):
    return (jnp.arange(block_total)[:, None] == (column_ids // BLOCK)[None, :]).astype(jnp.float32)


def row_table(panel_rows, block_rows):
    row_ids = jnp.arange(panel_rows)
    return ((row_ids // BLOCK)[:, None] == jnp.arange(block_rows)[None, :]).astype(jnp.float32)


def general(
    frames_in,
    kept_state,
    moved_to,
    xz_weight,
    side_weight,
    xz_mask,
    dt_bias,
    decay_rate,
    skip_gain,
    norm_gain,
    out_weight,
    out_mask,
):
    device_count = lax.axis_size("stream")
    shard_pos = lax.axis_index("shard")
    slots = kept_state.shape[0]
    target_dev = moved_to // slots
    target_slot = moved_to % slots
    slot_ids = jnp.arange(slots)
    same_dest = (target_dev[:, None] == target_dev[None, :]) & (
        slot_ids[:, None] > slot_ids[None, :]
    )
    ranking = jnp.sum(same_dest.astype(jnp.int32), axis=1)
    position = target_dev * MOST + ranking
    send_states = (
        jnp.zeros((device_count * MOST,) + kept_state.shape[1:], jnp.float32)
        .at[position]
        .set(kept_state)
    )
    send_slots = jnp.full((device_count * MOST,), -1, jnp.int32).at[position].set(target_slot)
    got_states, got_slots = (
        lax.all_to_all(
            send_states.astype(jnp.bfloat16), "stream", split_axis=0, concat_axis=0, tiled=True
        ).astype(send_states.dtype),
        lax.all_to_all(send_slots, "stream", split_axis=0, concat_axis=0, tiled=True),
    )
    landing = jnp.where(got_slots >= 0, got_slots, slots)
    carry_state = jnp.zeros_like(kept_state).at[landing].set(got_states, mode="drop")
    patch_len = frames_in.shape[2]
    local_rows = frames_in.reshape(-1, frames_in.shape[3])
    features = lax.all_gather(local_rows, "shard", axis=1, tiled=True)
    row_count = features.shape[0]
    width_local = xz_weight.shape[2]
    block_rows = xz_mask.shape[0]
    column_ids = shard_pos * width_local + jnp.arange(width_local)
    col_onehot = column_table(column_ids, xz_mask.shape[2])
    xz_keep = jnp.einsum("rgc,cl->rgl", xz_mask.astype(jnp.float32), col_onehot).reshape(
        block_rows, 2 * width_local
    )
    out_keep = jnp.dot(out_mask.astype(jnp.float32), col_onehot)
    panel = lax.all_gather(xz_weight, "stream", axis=0, tiled=True)
    panel_rows = panel.shape[0]
    keep_mask = jnp.dot(row_table(panel_rows, block_rows), xz_keep).astype(jnp.bfloat16)
    masked = panel.reshape(panel_rows, 2 * width_local) * keep_mask
    columns = features
    xz_total = jnp.dot(columns, masked, preferred_element_type=jnp.float32)
    columns = features
    side_total = jnp.dot(
        columns,
        lax.all_gather(side_weight, "stream", axis=0, tiled=True),
        preferred_element_type=jnp.float32,
    )
    head_count = dt_bias.shape[0]
    head_size = width_local // head_count
    head_inputs = xz_total[:, :width_local].reshape(slots, FRAMES, patch_len, head_count, head_size)
    gate_inputs = xz_total[:, width_local:]
    input_mix = side_total[:, :NSTATE].reshape(slots, FRAMES, patch_len, NSTATE)
    output_mix = side_total[:, NSTATE : 2 * NSTATE].reshape(slots, FRAMES, patch_len, NSTATE)
    step_raw = lax.dynamic_slice_in_dim(
        side_total, 2 * NSTATE + shard_pos * head_count, head_count, 1
    )
    step_sizes = jax.nn.softplus(step_raw + dt_bias).reshape(slots, FRAMES, patch_len, head_count)
    results = []
    for frame_index in range(FRAMES):
        outputs, carry_state = frame_step(
            head_inputs[:, frame_index],
            input_mix[:, frame_index],
            output_mix[:, frame_index],
            step_sizes[:, frame_index],
            decay_rate,
            skip_gain,
            carry_state,
        )
        results.append(outputs)
    scanned = jnp.stack(results, axis=1).reshape(row_count, width_local)
    gated = (scanned * jax.nn.silu(gate_inputs)).reshape(row_count, -1, DINNER // NORM_GROUPS)
    mean_square = jnp.mean(gated * gated, axis=2, keepdims=True)
    normed = (
        (gated * lax.rsqrt(mean_square + 1e-05)).reshape(row_count, width_local) * norm_gain
    ).astype(jnp.bfloat16)
    panel = lax.all_gather(out_weight, "stream", axis=0, tiled=True)
    panel_rows = panel.shape[0]
    keep_mask = jnp.dot(row_table(panel_rows, block_rows), out_keep).astype(jnp.bfloat16)
    partial_out = lax.dot_general(
        normed, panel * keep_mask, (((1,), (1,)), ((), ())), preferred_element_type=jnp.float32
    )
    mixed = lax.psum_scatter(
        partial_out.astype(jnp.bfloat16), "shard", scatter_dimension=1, tiled=True
    )
    return (mixed.reshape(slots, FRAMES, patch_len, -1), carry_state)


HEADDIM = 64
XZ_SHARE = 0.66
OUT_SHARE = 0.72
BF16 = jnp.bfloat16
F32 = jnp.float32
MIB = 1 << 20


def params(limit=48 * MIB):
    return pltpu.CompilerParams(vmem_limit_bytes=limit)


def cost():
    return pl.CostEstimate(flops=1, bytes_accessed=1, transcendentals=0)


def dot_nt(left, right):
    return lax.dot_general(left, right, (((1,), (1,)), ((), ())), preferred_element_type=F32)


def pack_kernel(block_rows, groups, columns, mask_columns, low_count, room, always, turn, at_ref, mask_ref, x_ref, *rest):
    out_ref = rest[-1]
    panel, shard = at_ref[0], at_ref[1]
    base = 0
    if low_count == 0:
        base = 1 + block_rows * always
        out_ref[0] = jnp.zeros((BLOCK, BLOCK), BF16)
        for row in range(block_rows):
            for column in range(always):
                block = rest[0][column * BLOCK : (column + 1) * BLOCK, row * BLOCK : (row + 1) * BLOCK].T
                short = BLOCK - block.shape[1]
                if short:
                    block = jnp.concatenate([block, jnp.zeros((BLOCK, short), BF16)], axis=1)
                out_ref[1 + row * always + column] = block
    count = jnp.int32(-low_count)
    for row in range(block_rows):
        for group in range(groups):
            for column in range(columns):
                place = ((panel * block_rows + row) * groups + group) * mask_columns + shard * columns + column
                keep = mask_ref[place] != 0
                low = (group * columns + column) * BLOCK

                @pl.when(keep & (count >= 0) & (count < room))
                def _(count=count, low=low, row=row):
                    block = x_ref[row * BLOCK : (row + 1) * BLOCK, low : low + BLOCK]
                    out_ref[base + count] = block.T if turn else block

                count = count + keep.astype(jnp.int32)


def pack(at, mask, panel, groups, low_count, room, turn, beside=None):
    rows, width = panel.shape
    columns = width // groups // BLOCK
    always = 0 if beside is None else -(-beside.shape[0] // BLOCK)
    smem = pl.BlockSpec(memory_space=pltpu.SMEM)
    vmem = pl.BlockSpec(memory_space=pltpu.VMEM)
    extra = () if beside is None else (beside,)
    size = room if low_count else 1 + rows // BLOCK * always + room
    return pl.pallas_call(
        functools.partial(
            pack_kernel, rows // BLOCK, groups, columns, mask.shape[-1], low_count, room, always, turn
        ),
        out_shape=jax.ShapeDtypeStruct((size, BLOCK, BLOCK), BF16),
        in_specs=[smem, smem, vmem] + [vmem] * len(extra),
        out_specs=vmem,
        compiler_params=params(),
        cost_estimate=cost(),
    )(at, mask.reshape(-1), panel, *extra)


def unwritten(shape):
    return pl.pallas_call(
        lambda out_ref: None,
        out_shape=jax.ShapeDtypeStruct(shape, BF16),
        out_specs=pl.BlockSpec(memory_space=pl.ANY),
        cost_estimate=cost(),
    )()


def slot_table(mask, panels, shard, shards, always):
    rows = mask.shape[0] // panels
    mine = lax.dynamic_slice_in_dim(mask, shard * (mask.shape[-1] // shards), mask.shape[-1] // shards, mask.ndim - 1)
    kept = mine.reshape(panels, -1)
    size = kept.shape[1]
    before = (jnp.arange(size)[:, None] < jnp.arange(size)[None, :]).astype(F32)
    rank = jnp.dot(kept.astype(F32), before).astype(jnp.int32)
    table = jnp.where(kept != 0, rank + 1 + rows * always, 0).reshape(panels, rows, -1)
    fixed = 1 + jnp.arange(rows)[:, None] * always + jnp.arange(always)[None, :]
    fixed = jnp.broadcast_to(fixed[None], (panels, rows, always)).astype(jnp.int32)
    return jnp.concatenate([table, fixed], axis=2).reshape(-1)


def panel_copies(parts, over, panel, held, sems):
    copies, low = [], 0
    for i, part in enumerate(parts):
        copies.append(pltpu.make_async_copy(part, held.at[pl.ds(low, part.shape[0])], sems.at[i]))
        low += part.shape[0]
    return copies, pltpu.make_async_copy(over.at[panel], held.at[pl.ds(low, over.shape[1])], sems.at[2])


def project_kernel(counts, block_rows, blocks, tiles, at_ref, table_ref, x_ref, over_ref, *refs):
    out_ref, held, x_held, *dense, total, sems, x_sems, out_sems = refs[len(refs) - 9 :]
    parts, low = [], 0
    for count in counts:
        parts.append(refs[low : low + count])
        low += count
    me, extra = at_ref[0], at_ref[2] != 0
    depth = block_rows * BLOCK
    pairs = len(counts) // 2

    def fetch(pair):
        slot, plain, more = pair % 2, [], []
        for side in range(2):
            panel = me ^ (2 * pair + side)
            copies, over = panel_copies(
                parts[2 * pair + side], over_ref, panel, held.at[slot, side], sems.at[slot, side]
            )
            columns = pl.ds(pl.multiple_of(panel * depth, BLOCK), depth)
            copies.append(
                pltpu.make_async_copy(
                    x_ref.at[:, columns], x_held.at[slot, :, pl.ds(side * depth, depth)], x_sems.at[slot, side]
                )
            )
            plain += copies
            more.append(over)
        return plain, more

    def start(pair):
        plain, more = fetch(pair)
        for copy in plain:
            copy.start()

        @pl.when(extra)
        def _():
            for copy in more:
                copy.start()

    def wait(pair):
        plain, more = fetch(pair)
        for copy in plain:
            copy.wait()

        @pl.when(extra)
        def _():
            for copy in more:
                copy.wait()

    def out_copy(n):
        first, size = tiles[n]
        columns = pl.ds(first * BLOCK, size * BLOCK)
        return pltpu.make_async_copy(total.at[:, columns], out_ref.at[:, columns], out_sems.at[n])

    def fill(pair, n):
        first, size = tiles[n]
        for side in range(2):
            panel = me ^ (2 * pair + side)
            for row in range(block_rows):
                line = (panel * block_rows + row) * blocks + first
                high = (side * block_rows + row) * BLOCK
                for column in range(size):
                    dense[n % 2][high : high + BLOCK, column * BLOCK : (column + 1) * BLOCK] = held[
                        pair % 2, side, table_ref[line + column]
                    ]

    def multiply(pair, n):
        first, size = tiles[n]
        columns = slice(first * BLOCK, (first + size) * BLOCK)
        term = jnp.dot(x_held[pair % 2], dense[n % 2][:, : size * BLOCK], preferred_element_type=F32)
        total[:, columns] = term + jnp.where(pair > 0, total[:, columns], 0.0)

    start(0)

    @pl.loop(0, pairs)
    def _(pair):
        for i in range(pairs):

            @pl.when(pair == i)
            def _(i=i):
                wait(i)
                if i + 1 < pairs:
                    start(i + 1)

        fill(pair, 0)
        for n in range(len(tiles)):
            if n + 1 < len(tiles):
                fill(pair, n + 1)
            multiply(pair, n)

            @pl.when(pair == pairs - 1)
            def _(n=n):
                out_copy(n).start()

    for n in range(len(tiles)):
        out_copy(n).wait()


def project(at, table, features, panels, over, block_rows, wide=4):
    rows = features.shape[0]
    count = len(panels)
    blocks = table.shape[0] // (count * block_rows)
    size = sum(part.shape[0] for part in panels[0]) + over.shape[1]
    flat = [part for bits in range(count) for part in panels[bits]]
    smem = pl.BlockSpec(memory_space=pltpu.SMEM)
    anywhere = pl.BlockSpec(memory_space=pl.ANY)
    depth = 2 * block_rows * BLOCK
    tiles = [(first, min(wide, blocks - first)) for first in range(0, blocks, wide)]
    return pl.pallas_call(
        functools.partial(project_kernel, [len(panels[b]) for b in range(count)], block_rows, blocks, tiles),
        out_shape=jax.ShapeDtypeStruct((rows, blocks * BLOCK), F32),
        in_specs=[smem, smem] + [anywhere] * (2 + len(flat)),
        out_specs=anywhere,
        scratch_shapes=[
            pltpu.VMEM((2, 2, size, BLOCK, BLOCK), BF16),
            pltpu.VMEM((2, rows, depth), BF16),
            pltpu.VMEM((depth, wide * BLOCK), BF16),
            pltpu.VMEM((depth, wide * BLOCK), BF16),
            pltpu.VMEM((rows, blocks * BLOCK), F32),
            pltpu.SemaphoreType.DMA((2, 2, 3)),
            pltpu.SemaphoreType.DMA((2, 2)),
            pltpu.SemaphoreType.DMA((len(tiles),)),
        ],
        compiler_params=params(56 * MIB),
        cost_estimate=cost(),
    )(at, table, features, over, *flat)


def pick_kernel(order_ref, x_ref, out_ref):
    out_ref[...] = x_ref[...].astype(out_ref.dtype)


def pick(order, states):
    count, block = order.shape[0], (1,) + states.shape[1:]
    return pl.pallas_call(
        pick_kernel,
        grid_spec=pltpu.PrefetchScalarGridSpec(
            num_scalar_prefetch=1,
            grid=(count,),
            in_specs=[pl.BlockSpec(block, lambda i, order: (order[i], 0, 0))],
            out_specs=pl.BlockSpec(block, lambda i, order: (i, 0, 0)),
        ),
        out_shape=jax.ShapeDtypeStruct((count,) + states.shape[1:], BF16),
        compiler_params=params(),
        cost_estimate=cost(),
    )(order, states)


def split(values):
    high = values.astype(BF16)
    left = values - high.astype(F32)
    middle = left.astype(BF16)
    return high, middle, (left - middle.astype(F32)).astype(BF16)


def scan_kernel(heads, group_width, slots_ref, total_ref, state_ref, rows_ref, heads_ref, pick_ref, *rest):
    normed_ref, carry_ref = rest[-2:]
    length, width = normed_ref.shape
    head_inputs = total_ref[:, :width]
    gate_inputs = total_ref[:, width : 2 * width]
    side = 2 * width
    input_mix = total_ref[:, side : side + NSTATE].astype(BF16)
    output_mix = total_ref[:, side + NSTATE : side + 2 * NSTATE].astype(BF16)
    bias, decay = heads_ref[0:1, :], heads_ref[1:2, :]
    skip, gain = rows_ref[0:1, :], rows_ref[1:2, :]
    raw = total_ref[:, side + 2 * NSTATE : side + 2 * NSTATE + heads_ref.shape[1]] + bias
    steps = jnp.maximum(raw, 0.0) + jnp.log1p(jnp.exp(-jnp.abs(raw)))
    patch = length // FRAMES

    def token(shape, axis, size):
        row = lax.broadcasted_iota(jnp.int32, shape, axis) & (size - 1)
        return (row & (FRAMES - 1)) * patch + row // FRAMES

    square = (length, length)
    lower = (token(square, 0, 64) >= token(square, 1, 64)).astype(BF16)
    cumulative = sum(jnp.dot(lower, part, preferred_element_type=F32) for part in split(-(steps * decay)))
    both = jnp.concatenate(split(jnp.concatenate([steps, cumulative], axis=0)), axis=1)
    both = jnp.dot(both, pick_ref[...], preferred_element_type=F32)
    steps, cumulative = both[:length], both[length:]
    lane = lax.broadcasted_iota(jnp.int32, (length, width), 1) & (HEADDIM - 1)
    line = lax.broadcasted_iota(jnp.int32, (length, width), 0)
    own = lane == line
    cum_row = jnp.sum(jnp.where(own, cumulative, 0.0), axis=0, keepdims=True)
    step_row = jnp.sum(jnp.where(own, steps, 0.0), axis=0, keepdims=True)
    last = cumulative[length - 1 : length, :]
    causal = (token((length, width), 1, HEADDIM) <= token((length, width), 0, 64)) & (lane < length)
    mixing = jnp.exp(jnp.where(causal, cumulative - cum_row, -1e30)) * step_row
    half = lax.broadcasted_iota(jnp.int32, (length, 2 * HEADDIM), 1) < HEADDIM
    spare = jnp.zeros((HEADDIM - length, NSTATE), BF16)
    twice = jnp.concatenate([input_mix, spare, input_mix, spare], axis=0)
    scores = dot_nt(output_mix, twice)
    inputs16 = head_inputs.astype(BF16)
    inside = []
    for pair in range(heads // 2):
        low = pair * 2 * HEADDIM
        inputs = inputs16[:, low : low + 2 * HEADDIM]
        zero = jnp.zeros_like(inputs)
        pad = jnp.zeros((HEADDIM - length, 2 * HEADDIM), BF16)
        both = jnp.concatenate([jnp.where(half, inputs, zero), pad, jnp.where(half, zero, inputs), pad], axis=0)
        mix = (mixing[:, low : low + 2 * HEADDIM] * scores).astype(BF16)
        inside.append(jnp.dot(mix, both, preferred_element_type=F32))
    inside = jnp.concatenate(inside, axis=1)
    state = state_ref[0]
    carried = jnp.exp(cumulative) * dot_nt(output_mix, state)
    scanned = inside + carried + skip * head_inputs
    gated = scanned * (gate_inputs / (1.0 + jnp.exp(-gate_inputs)))
    channel = lax.broadcasted_iota(jnp.int32, (width, 128), 0)
    member = lax.broadcasted_iota(jnp.int32, (width, 128), 1) * group_width
    member = ((channel >= member) & (channel < member + group_width)).astype(BF16)
    squares = jnp.dot((gated * gated).astype(BF16), member, preferred_element_type=F32)
    scale = lax.rsqrt(squares * (1.0 / group_width) + 1e-05)
    position = lax.broadcasted_iota(jnp.int32, (length, width), 1)
    spread_scale = jnp.broadcast_to(scale[:, 0:1], (length, width))
    for group in range(1, width // group_width):
        spread_scale = jnp.where(position >= group * group_width, scale[:, group : group + 1], spread_scale)
    normed_ref[...] = (gated * spread_scale * gain).astype(BF16)
    to_end = (jnp.exp(last - cumulative) * steps * head_inputs).astype(BF16)
    added = lax.dot_general(to_end, input_mix, (((0,), (0,)), ((), ())), preferred_element_type=F32)
    head_rows = -(-heads // 8) * 8
    head_of = lax.broadcasted_iota(jnp.int32, (head_rows, width), 1)
    first = lax.broadcasted_iota(jnp.int32, (head_rows, width), 0) * HEADDIM
    whole = jnp.sum(jnp.where(head_of == first, last, 0.0), axis=1, keepdims=True)
    whole = jnp.broadcast_to(jnp.exp(whole), (head_rows, NSTATE))
    for head in range(heads):
        rows = slice(head * HEADDIM, (head + 1) * HEADDIM)
        carry_ref[0, rows, :] = state[rows].astype(F32) * whole[head : head + 1, :] + added[rows]


def scan(slots, total, state, rows, per_head, picked, carry, total_slots, group_width):
    count, width, _ = state.shape
    length = total.shape[0] // total_slots
    more = [] if carry is None else [pl.BlockSpec(memory_space=pl.ANY)]
    return pl.pallas_call(
        functools.partial(scan_kernel, width // HEADDIM, group_width),
        grid_spec=pltpu.PrefetchScalarGridSpec(
            num_scalar_prefetch=1,
            grid=(count,),
            in_specs=[
                pl.BlockSpec((length, total.shape[1]), lambda i, slots: (slots[i], 0)),
                pl.BlockSpec((1, width, NSTATE), lambda i, slots: (i, 0, 0)),
                pl.BlockSpec(rows.shape, lambda i, slots: (0, 0)),
                pl.BlockSpec(per_head.shape, lambda i, slots: (0, 0)),
                pl.BlockSpec(picked.shape, lambda i, slots: (0, 0)),
            ]
            + more,
            out_specs=(
                pl.BlockSpec((length, width), lambda i, slots: (i, 0)),
                pl.BlockSpec((1, width, NSTATE), lambda i, slots: (slots[i], 0, 0)),
            ),
        ),
        out_shape=(
            jax.ShapeDtypeStruct((count * length, width), BF16),
            jax.ShapeDtypeStruct((total_slots, width, NSTATE), F32),
        ),
        input_output_aliases={} if carry is None else {6: 1},
        compiler_params=params(),
        cost_estimate=cost(),
    )(slots, total, state, rows, per_head, picked, *(() if carry is None else (carry,)))


def expand_terms_kernel(counts, block_rows, blocks, first_pair, at_ref, table_ref, normed_ref, over_ref, *refs):
    term_ref, dense_ref, held, sems = refs[len(refs) - 4 :]
    me, extra = at_ref[0], at_ref[2] != 0
    pairs = len(counts) // 2
    step = pl.program_id(0)

    def each(number, act):
        slot = number % 2
        for pair in range(pairs):
            low = sum(counts[: 2 * pair])

            @pl.when(number == pair)
            def _(pair=pair, low=low):
                for side in range(2):
                    parts = refs[low : low + counts[2 * pair + side]]
                    low += counts[2 * pair + side]
                    panel = me ^ (2 * (first_pair + pair) + side)
                    plain, over = panel_copies(parts, over_ref, panel, held.at[slot, side], sems.at[slot, side])
                    for copy in plain:
                        act(copy)

                    @pl.when(extra)
                    def _(over=over):
                        act(over)

    @pl.when(step == 0)
    def _():
        each(0, lambda copy: copy.start())

    @pl.when(step + 1 < pairs)
    def _():
        each(step + 1, lambda copy: copy.start())

    each(step, lambda copy: copy.wait())
    for side in range(2):
        panel = me ^ (2 * (first_pair + step) + side)
        place = (panel % 2) * (block_rows * BLOCK)
        for row in range(block_rows):
            columns = pl.ds(pl.multiple_of(place + row * BLOCK, BLOCK), BLOCK)
            line = (panel * block_rows + row) * blocks
            for column in range(blocks):
                dense_ref[0, column * BLOCK : (column + 1) * BLOCK, columns] = held[
                    step % 2, side, table_ref[line + column]
                ]
    term_ref[...] = jnp.dot(normed_ref[...], dense_ref[0], preferred_element_type=F32).astype(BF16)


def expand_terms(at, table, normed, panels, over, first_pair, pairs, block_rows, before):
    rows, depth = normed.shape
    count = over.shape[0]
    blocks = table.shape[0] // (count * block_rows)
    chosen = [panels[2 * first_pair + i] for i in range(2 * pairs)]
    flat = [part for parts in chosen for part in parts]
    size = sum(part.shape[0] for part in chosen[0]) + over.shape[1]
    anywhere = pl.BlockSpec(memory_space=pl.ANY)
    width = 2 * block_rows * BLOCK
    more = [] if before is None else list(before)

    def dest(i, at):
        return (at[0] // 2) ^ (first_pair + i)

    return pl.pallas_call(
        functools.partial(expand_terms_kernel, [len(parts) for parts in chosen], block_rows, blocks, first_pair),
        grid_spec=pltpu.PrefetchScalarGridSpec(
            num_scalar_prefetch=2,
            grid=(pairs,),
            in_specs=[pl.BlockSpec((rows, depth), lambda i, at, table: (0, 0))]
            + [anywhere] * (1 + len(flat) + len(more)),
            out_specs=(
                pl.BlockSpec((rows, width), lambda i, at, table: (0, dest(i, at))),
                pl.BlockSpec((1, depth, width), lambda i, at, table: (dest(i, at), 0, 0)),
            ),
            scratch_shapes=[
                pltpu.VMEM((2, 2, size, BLOCK, BLOCK), BF16),
                pltpu.SemaphoreType.DMA((2, 2, 3)),
            ],
        ),
        out_shape=(
            jax.ShapeDtypeStruct((rows, count // 2 * width), BF16),
            jax.ShapeDtypeStruct((count // 2, depth, width), BF16),
        ),
        input_output_aliases={4 + len(flat): 0, 5 + len(flat): 1} if more else {},
        compiler_params=params(),
        cost_estimate=cost(),
    )(at, table, normed, over, *flat, *more)


def terms_kernel(normed_ref, dense_ref, out_ref):
    out_ref[...] = jnp.dot(normed_ref[...], dense_ref[0], preferred_element_type=F32).astype(BF16)


def terms(normed, dense):
    rows, depth = normed.shape
    shards, _, width = dense.shape
    return pl.pallas_call(
        terms_kernel,
        grid=(shards,),
        in_specs=[
            pl.BlockSpec((rows, depth), lambda i: (0, 0)),
            pl.BlockSpec((1, depth, width), lambda i: (i, 0, 0)),
        ],
        out_specs=pl.BlockSpec((rows, width), lambda i: (0, i)),
        out_shape=jax.ShapeDtypeStruct((rows, shards * width), BF16),
        compiler_params=params(),
        cost_estimate=cost(),
    )(normed, dense)


def add(got, term):
    return (got.astype(F32) + term.astype(F32)).astype(BF16)


def place_kernel(slots_ref, got_ref, *rest):
    out_ref = rest[-1]
    total = got_ref[...].astype(F32)
    patch, frames = out_ref.shape[1:3]
    for token in range(patch):
        out_ref[0, token] = total[token * frames : (token + 1) * frames].astype(BF16)


def place(slots, got, total_slots, before):
    rows, width = got.shape
    count = slots.shape[0]
    patch = rows // count // FRAMES
    return pl.pallas_call(
        place_kernel,
        grid_spec=pltpu.PrefetchScalarGridSpec(
            num_scalar_prefetch=1,
            grid=(count,),
            in_specs=[pl.BlockSpec((rows // count, width), lambda i, slots: (i, 0))]
            + ([] if before is None else [pl.BlockSpec(memory_space=pl.ANY)]),
            out_specs=pl.BlockSpec((1, patch, FRAMES, width), lambda i, slots: (slots[i], 0, 0, 0)),
        ),
        out_shape=jax.ShapeDtypeStruct((total_slots, patch, FRAMES, width), BF16),
        input_output_aliases={} if before is None else {2: 0},
        compiler_params=params(),
        cost_estimate=cost(),
    )(slots, got, *(() if before is None else (before,)))


def swap(value, bit, size):
    return lax.ppermute(value, "stream", [(i, i ^ bit) for i in range(size)])


def cube(own, size):
    return {0: [own], 2: [swap(own, 2, size)], 4: [swap(own, 4, size)], 1: [swap(own, 1, size)]}


def cube_rest(got, size, near):
    half = got[0][0].shape[0] // 2
    got[6] = [swap(got[4][0][:half], 2, size), swap(got[2][0][half:], 4, size)]
    for bits in near:
        got[bits | 1] = [swap(part, 1, size) for part in got[bits]]
    return got


def after(values, earlier):
    return lax.optimization_barrier((values, earlier))[0]


def sparse(
    frames_in,
    kept_state,
    moved_to,
    xz_weight,
    side_weight,
    xz_mask,
    dt_bias,
    decay_rate,
    skip_gain,
    norm_gain,
    out_weight,
    out_mask,
):
    streams, shards = lax.axis_size("stream"), lax.axis_size("shard")
    me, shard = lax.axis_index("stream"), lax.axis_index("shard")
    slots, heads = kept_state.shape[:2]
    width = heads * HEADDIM
    block_rows = out_weight.shape[0] // BLOCK
    out_blocks = block_rows * (width // BLOCK)
    xz_room, out_room = int(2 * out_blocks * XZ_SHARE), int(out_blocks * OUT_SHARE)
    at = jnp.stack([me, shard]).astype(jnp.int32)

    frames = frames_in.transpose(0, 2, 1, 3).reshape(-1, frames_in.shape[3])
    features = lax.all_gather(frames, "shard", axis=1, tiled=True)

    side_blocks = -(-side_weight.shape[1] // BLOCK)
    xz_panel = after(xz_weight, frames).reshape(xz_weight.shape[0], -1)
    xz_packed = pack(at, xz_mask, xz_panel, 2, 0, xz_room, False, side_weight.T)
    xz_panels = cube(xz_packed, streams)

    steps = (1, 2, 3, streams // 2)
    match = (moved_to // slots - me) % streams == jnp.array(steps)[:, None]
    rank = jnp.cumsum(match.astype(jnp.int32), axis=1) - 1
    chosen = match[:, None, :] & (rank[:, None, :] == jnp.arange(MOST)[None, :, None])
    order = jnp.sum(jnp.where(chosen, jnp.arange(slots), 0), axis=2, dtype=jnp.int32)
    landing = jnp.sum(jnp.where(chosen, moved_to % slots, 0), axis=2, dtype=jnp.int32)

    def move(values, k):
        return lax.ppermute(values, "stream", [(i, (i + steps[k]) % streams) for i in range(streams)])

    landing = [move(after(landing, xz_packed)[k], k) for k in range(len(steps))]
    order = after(order, xz_packed)
    flat_state = kept_state.reshape(slots, width, NSTATE)
    sends = [pick(order[k], flat_state) for k in range(len(steps))]
    out_packed = pack(at, after(out_mask, xz_packed), out_weight, 1, 0, out_room, True)
    masks = after((xz_mask, out_mask), sends)
    kept_xz, kept_out = (fullest(mask, streams, shards) for mask in masks)
    xz_table = slot_table(xz_mask, streams, shard, shards, side_blocks)
    out_table = slot_table(out_mask, streams, shard, shards, 0)
    head_of = jnp.arange(width) // HEADDIM
    picked = (shard * heads + head_of[None, :] == jnp.arange(BLOCK)[:, None]).astype(BF16)
    picked = jnp.concatenate([picked] * 3, axis=0)
    per_head = jnp.zeros((8, BLOCK), F32)
    per_head = lax.dynamic_update_slice(per_head, jnp.stack([dt_bias, decay_rate]), (0, shard * heads))
    rows = jnp.stack([jnp.repeat(skip_gain, HEADDIM), norm_gain] + [jnp.zeros_like(norm_gain)] * 6)

    (xz_panels[2], xz_panels[4], sends[0]) = after(
        (xz_panels[2], xz_panels[4], sends[0]), (xz_panels[1], sends, out_packed, kept_xz, kept_out, xz_table, out_table, picked, per_head, rows, landing)
    )
    got = [move(sends[0], 0)]
    xz_panels = cube_rest(xz_panels, streams, (2, 4, 6))

    out_packed = after(out_packed, xz_panels[6])
    out_panels = cube(out_packed, streams)
    extra = after((kept_xz > xz_room) | (kept_out > out_room), (xz_panels[6], features, got))
    spare_xz, spare_out = 2 * out_blocks - xz_room, out_blocks - out_room

    def none(*_):
        return unwritten((streams, spare_xz, BLOCK, BLOCK)), unwritten((streams, spare_out, BLOCK, BLOCK))

    def some(xz_panel, out_weight):
        over_xz = pack(at, xz_mask, xz_panel, 2, xz_room, spare_xz, False)
        over_out = pack(at, out_mask, out_weight, 1, out_room, spare_out, True)
        return tuple(lax.all_gather(over, "stream", axis=0) for over in (over_xz, over_out))

    over_xz, over_out = lax.cond(extra, some, none, xz_panel, out_weight)
    at = jnp.concatenate([at, extra.astype(jnp.int32)[None]])
    total = project(at, xz_table, features, xz_panels, over_xz, block_rows)
    out_panels, total = lax.optimization_barrier((out_panels, total))
    out_panels = cube_rest(out_panels, streams, (2, 4))
    sends[1:] = after(sends[1:], out_panels[6])
    got.append(move(sends[1], 1))
    got += [move(sends[k], k) for k in range(2, len(steps))]

    pairs = streams // 2
    count = len(steps)

    def scan_chunk(k, total, carry):
        return scan(landing[k], total, got[k], rows, per_head, picked, carry, slots, DINNER // NORM_GROUPS)

    done, carry = scan_chunk(0, total, None)
    most = expand_terms(at, out_table, done, out_panels, over_out, 0, pairs - 1, block_rows, None)
    last = after(out_panels[2 * pairs - 2], most)
    out_panels[2 * pairs - 2] = last
    out_panels[2 * pairs - 1] = [swap(part, 1, streams) for part in last]
    term, dense = expand_terms(at, out_table, done, out_panels, over_out, pairs - 1, 1, block_rows, most)

    ring = [(i, (i + 1) % shards) for i in range(shards)]

    def term_for(k, hop):
        return lax.dynamic_slice_in_dim(terms_of[k], (shard - hop) % shards * width, width, 1)

    mixed, moving, terms_of = None, [], [term]
    for step in range(count + shards - 1):
        if step < count:
            if step:
                done, carry = scan_chunk(step, total, carry)
                terms_of.append(terms(done, dense))
            moving.append(lax.ppermute(term_for(step, 1), "shard", ring))
        passed = []
        for k in range(max(step - shards + 1, 0), min(step, count)):
            hop = step - k + 1
            value = add(moving[k], term_for(k, hop))
            passed.append(value)
            if hop < shards:
                moving[k] = lax.ppermute(value, "shard", ring)
            else:
                mixed = place(landing[k], value, slots, mixed)
        total = after(total, (terms_of[-1], passed))
    return mixed.transpose(0, 2, 1, 3), carry.reshape(kept_state.shape)


def fullest(mask, panels, shards):
    rows = mask.reshape(panels, -1, mask.shape[-1])
    cells = rows.reshape(panels, rows.shape[1], shards, -1)
    return jnp.max(jnp.sum(cells, axis=(1, 3)))


def on_device(streams, shards, *args):
    xz_weight, out_weight, kept_state = args[3], args[10], args[1]
    rows, width = out_weight.shape
    regular = (
        streams == 8
        and streams % shards == 0
        and rows % BLOCK == 0
        and width % BLOCK == 0
        and width % (DINNER // NORM_GROUPS) == 0
        and width == (streams // shards) * rows
        and streams // shards == 2
        and args[9].shape[0] == width
        and kept_state.shape[1] % 2 == 0
    )
    if not regular:
        return general(*args)
    return sparse(*args)


def solution(mesh):
    placed = (
        P("stream", None, None, "shard"),
        P("stream", "shard", None, None),
        P("stream"),
        P("stream", None, "shard"),
        P("stream", None),
        P(),
        P("shard"),
        P("shard"),
        P("shard"),
        P("shard"),
        P("stream", "shard"),
        P(),
    )
    return jax.shard_map(
        functools.partial(on_device, mesh.shape["stream"], mesh.shape["shard"]),
        mesh=mesh,
        in_specs=placed,
        out_specs=(P("stream", None, None, "shard"), P("stream", "shard", None, None)),
        check_vma=False,
    )
```
